512 devices in a mesh: tm: 8 (over x, core), row: 64 (over y, z).
Axes of the slice: x: 4, y: 8, z: 8, core: 2. Of those that a mesh axis runs over, the one named last changes fastest.
Arguments:
- forcing: float32 [8, 2048, 2048], P('tm', 'row'), may hold values from -6 to 6
- rate_class: int32 [2048, 2048], P('row'), may hold values from 0 to 15
- rate_table: float32 [16], replicated, may hold values from 0.95 to 0.999
- row_class: int32 [2048], replicated, may hold values from 0 to 1
- col_class: int32 [2048], replicated, may hold values from 0 to 1
- inverse_offsets: float32 [2, 512, 512], P(None, 'row'), may hold values from -0.25 to 0.25
Outputs:
- covariance_field: float32 [8, 2048, 2048], P('tm', 'row')
- adjoint_field: float32 [8, 2048, 2048], P('tm', 'row')
The draws below stay inside these ranges and needn't reach their ends.
All inputs are finite; a program needn't handle non-finite values.
Results may differ from the reference program's by a relative error of at most 0.0001.
Values sent between devices are 32-bit elements; how exact they have to be, the bound alone decides.
No kernel may reach another device: no remote copies, remote signals or barrier semaphores. Data moves between devices by JAX's collectives and lax.ppermute only.
A program may use at most 64 MiB of HBM per device.

```python
import jax
import jax.numpy as jnp
from jax import lax

GRID = 2048
BLOCK = 512
CLASSES = 2
RATES = 16
STEPS = 8


def touch_ends(values, own_key, least, top_value):
    dims = values.shape
    index_at = [jax.random.randint(jax.random.fold_in(own_key, axis), (), 0, dims[axis]) for axis in range(len(dims))]
    values = values.at[tuple(index_at)].set(least)
    longest = dims.index(max(dims))
    index_at[longest] = (index_at[longest] + 1) % dims[longest]
    return values.at[tuple(index_at)].set(top_value)


def block_scale(own_key, shape, cuts, low, largest):
    def one(dim, shards_of):
        steps = jax.random.uniform(jax.random.fold_in(jax.random.fold_in(own_key, 6), dim), (shards_of,), jnp.float32, low / len(cuts), largest / len(cuts))
        return jnp.repeat(jnp.exp(steps), shape[dim] // shards_of).reshape((-1,) + (1,) * (len(shape) - dim - 1))

    level = one(*cuts[0])
    for cut in cuts[1:]:
        level = level * one(*cut)
    return level


def scatter_about(own_key, extent, width, most, split=(), kind=jnp.bfloat16):
    array = width * jax.random.normal(own_key, extent, jnp.float32)
    if split:
        array = array * block_scale(own_key, extent, split, -0.22, 0.18)
    return jnp.clip(array, -most, most).astype(kind)


def setup_inputs(seed: int = 0) -> dict:
    splits = jax.random.split(jax.random.key(seed), 7)
    return {
        "forcing": scatter_about(splits[0], (STEPS, GRID, GRID), 1.0, 6.0, ((0, 8), (1, 64)), jnp.float32),
        "rate_class": touch_ends(jax.random.randint(splits[1], (GRID, GRID), 0, RATES), jax.random.fold_in(splits[1], 1), 0, RATES - 1).astype(jnp.int32),
        "rate_table": jnp.clip(jax.random.uniform(splits[2], (RATES,), jnp.float32, 0.95, 0.999), 0.95, 0.999),
        "row_class": touch_ends(jax.random.randint(splits[3], (GRID,), 0, CLASSES), jax.random.fold_in(splits[3], 1), 0, CLASSES - 1).astype(jnp.int32),
        "col_class": touch_ends(jax.random.randint(splits[4], (GRID,), 0, CLASSES), jax.random.fold_in(splits[4], 1), 0, CLASSES - 1).astype(jnp.int32),
        "inverse_offsets": scatter_about(splits[5], (CLASSES, BLOCK, BLOCK), BLOCK ** -0.5, 0.25, ((1, 64),), jnp.float32),
    }


def solve_rows(grid_field, matrices, labels, adjoint):
    pieces = grid_field.reshape(grid_field.shape[0], -1, matrices.shape[1])
    pattern = 'ybj,ij->ybi' if adjoint else 'ybi,ij->ybj'
    result = jnp.einsum(pattern, pieces, matrices[0], precision=lax.Precision.HIGHEST)
    for category in range(1, matrices.shape[0]):
        other = jnp.einsum(pattern, pieces, matrices[category], precision=lax.Precision.HIGHEST)
        result = jnp.where((labels == category)[:, None, None], other, result)
    return result.reshape(grid_field.shape)

def solve_columns(grid_field, matrices, labels, adjoint):
    pieces = grid_field.reshape(-1, matrices.shape[1], grid_field.shape[1])
    pattern = 'bjx,ij->bix' if adjoint else 'bix,ij->bjx'
    result = jnp.einsum(pattern, pieces, matrices[0], precision=lax.Precision.HIGHEST)
    for category in range(1, matrices.shape[0]):
        other = jnp.einsum(pattern, pieces, matrices[category], precision=lax.Precision.HIGHEST)
        result = jnp.where((labels == category)[None, None, :], other, result)
    return result.reshape(grid_field.shape)

def reference(forcing, rate_class, rate_table, row_class, col_class, inverse_offsets):
    matrices = inverse_offsets + jnp.eye(BLOCK, dtype=jnp.float32)[None]

    def forward_space(slab):
        return solve_columns(solve_rows(slab, matrices, row_class, False), matrices, col_class, False)

    def adjoint_space(slab):
        return solve_rows(solve_columns(slab, matrices, col_class, True), matrices, row_class, True)
    smoothed = lax.map(forward_space, forcing)
    decays = rate_table[rate_class]
    scaled = jnp.sqrt(1.0 - decays * decays)

    def advance(carried, source):
        carried = decays * carried + scaled * source
        return (carried, carried)
    start_state = jnp.zeros(decays.shape, jnp.float32)
    _, covariance_field = lax.scan(advance, start_state, smoothed)
    _, backward = lax.scan(advance, start_state, covariance_field, reverse=True)
    adjoint_field = lax.map(adjoint_space, backward)
    return (covariance_field, adjoint_field)
```

```python
import jax
import jax.numpy as jnp
from jax import lax
from jax.experimental import pallas as pl
from jax.experimental.pallas import tpu as pltpu
from jax.sharding import Mesh
from jax.sharding import PartitionSpec as P

BLOCK = 512
LANES = 128
PIECE = 32
F32 = jnp.float32
BF16 = jnp.bfloat16
ROWS = ("h", "l", "z")
TIME = ("x", "c")
SPREAD = ("x", "l", "z")


def split(values):
    high = values.astype(BF16)
    return high, (values - high.astype(F32)).astype(BF16)


def solve(lines, mask, highs, lows, adjoint):
    dims = (((1,), (1 if adjoint else 0,)), ((), ()))
    total = None
    for k in range(2):
        mine = lines * (mask if k == 0 else 1.0 - mask)
        high, low = split(mine)
        both = jnp.concatenate([high, low], axis=0)
        wide = lax.dot_general(both, highs[k], dims, preferred_element_type=F32)
        part = wide[: lines.shape[0]] + wide[lines.shape[0] :]
        part = part + lax.dot_general(high, lows[k], dims, preferred_element_type=F32)
        total = part if total is None else total + part
    return lines + total


def exchange_lanes(tiles):
    group = lax.broadcasted_iota(jnp.int32, tiles[0].shape, 1) // PIECE
    out = []
    for place in range(4):
        made = None
        for source in range(4):
            turn = ((source - place) % 4) * PIECE
            rolled = pltpu.roll(tiles[source], turn, 1) if turn else tiles[source]
            made = rolled if made is None else jnp.where(group == source, rolled, made)
        out.append(made)
    return out


def rows_kernel(f_ref, mine_ref, other_ref, mask_ref, out_ref, high_ref, low_ref):
    lines = jnp.concatenate(
        [
            f_ref[t, :, b * BLOCK : (b + 1) * BLOCK]
            for t in range(2)
            for b in range(2)
        ],
        axis=0,
    )
    for k, ref in enumerate((mine_ref, other_ref)):
        for s in range(4):
            high, low = split(ref[s])
            high_ref[k, :, s * LANES : (s + 1) * LANES] = high
            low_ref[k, :, s * LANES : (s + 1) * LANES] = low
    solved = solve(
        lines,
        mask_ref[...],
        [high_ref[0], high_ref[1]],
        [low_ref[0], low_ref[1]],
        False,
    )
    for s in range(4):
        turned = solved[:, s * LANES : (s + 1) * LANES].T
        out_ref[s * 16 : (s + 1) * 16] = turned.reshape(16, 8, LANES)


def middle_kernel(
    x_ref, rate_ref, mask_ref, table_ref, high_ref, low_ref, out_ref, a_ref, r_ref
):
    tiles = x_ref[...].reshape(4, 4, 4, 8, LANES)
    made = exchange_lanes([tiles[:, :, i].reshape(128, LANES) for i in range(4)])
    for tb in range(4):
        block = made[tb].reshape(4, 4, 8, LANES)
        for q in range(4):
            a_ref[:, tb, :, q * LANES : (q + 1) * LANES] = block[:, q]
    rates = rate_ref[...].reshape(4, 4, 8, LANES)
    made = exchange_lanes([rates[:, i].reshape(32, LANES) for i in range(4)])
    for b in range(2):
        block = made[b].reshape(4, 8, LANES)
        for q in range(4):
            r_ref[b, :, q * LANES : (q + 1) * LANES] = block[q]
    rate = r_ref[...].reshape(16, BLOCK)
    decays = jnp.zeros_like(rate)
    for k in range(16):
        decays = jnp.where(rate == float(k), table_ref[k], decays)
    scaled = jnp.sqrt(1.0 - decays * decays)

    highs, lows = [high_ref[0], high_ref[1]], [low_ref[0], low_ref[1]]
    mask = mask_ref[...]
    smoothed = solve(a_ref[...].reshape(128, BLOCK), mask, highs, lows, False)
    state, field = None, []
    for t in range(8):
        here = scaled * smoothed[t * 16 : (t + 1) * 16]
        state = here if state is None else decays * state + here
        field.append(state)
    state, back = None, [None] * 8
    for t in range(7, -1, -1):
        here = scaled * field[t]
        state = here if state is None else decays * state + here
        back[t] = state
    adjoint = solve(jnp.concatenate(back, axis=0), mask, highs, lows, True)
    field = jnp.concatenate(field, axis=0)
    for n, value in enumerate((field, adjoint)):
        parts = value.reshape(4, 4, 8, BLOCK)
        for q in range(4):
            tiles = [
                parts[:, tb, :, q * LANES : (q + 1) * LANES].reshape(32, LANES)
                for tb in range(4)
            ]
            made = exchange_lanes(tiles)
            for i in range(4):
                block = made[i].reshape(4, 8, LANES)
                for x in range(4):
                    out_ref[x * 16 + q * 4 + i, n * 8 : (n + 1) * 8, :] = block[x]


def last_kernel(x_ref, mask_ref, high_ref, low_ref, out_ref):
    pieces = [[], []]
    for s in range(4):
        for n in range(2):
            tile = x_ref[s * 16 : (s + 1) * 16, n * 8 : (n + 1) * 8, :]
            pieces[n].append(tile.reshape(LANES, LANES).T)
    field = jnp.concatenate(pieces[0], axis=1)
    lines = jnp.concatenate(pieces[1], axis=1)
    solved = solve(
        lines,
        mask_ref[...],
        [high_ref[0], high_ref[1]],
        [low_ref[0], low_ref[1]],
        True,
    )
    for n, value in enumerate((field, solved)):
        for t in range(2):
            for b in range(2):
                first = (t * 2 + b) * PIECE
                out_ref[t, n, :, b * BLOCK : (b + 1) * BLOCK] = value[
                    first : first + PIECE
                ]


def vmem(count):
    return [pl.BlockSpec(memory_space=pltpu.VMEM)] * count


PARAMS = pltpu.CompilerParams(vmem_limit_bytes=48 * 1024 * 1024)


def swap(values, axis):
    return lax.all_to_all(values, axis, split_axis=0, concat_axis=0, tiled=True)


def spread_out(values, axis):
    count = lax.axis_size(axis)
    return swap(jnp.broadcast_to(values[None], (count,) + values.shape), axis)


def gather_matrices(offsets, x, c):
    rows = offsets.shape[1]
    piece = lax.dynamic_slice(offsets, (c, 0, x * LANES), (1, rows, LANES))[0]
    slab = spread_out(piece, ROWS).reshape(BLOCK, LANES)
    mine = spread_out(slab, "x")
    other = lax.ppermute(mine, "c", [(0, 1), (1, 0)])
    return mine, other


def per_device(forcing, rate_class, rate_table, row_class, col_class, offsets):
    x, c = lax.axis_index("x"), lax.axis_index("c")
    place = lax.axis_index(("l", "z"))
    first_row = lax.axis_index(ROWS) * PIECE
    kind = c.astype(jnp.int32)

    my_rows = lax.dynamic_slice_in_dim(row_class, first_row, PIECE)
    row_mask = jnp.tile((my_rows == kind).astype(F32), 4).reshape(128, 1)
    columns = [c * 1024 + b * BLOCK + x * LANES for b in range(2)]
    my_cols = jnp.concatenate(
        [lax.dynamic_slice_in_dim(col_class, at + place * 8, 8) for at in columns]
    )
    col_mask = jnp.tile((my_cols == kind).astype(F32), 8).reshape(128, 1)

    f = forcing[0]
    f = swap(jnp.stack([f[:, :1024], f[:, 1024:]]), "c")
    rate = [lax.dynamic_slice(rate_class, (0, at), (PIECE, LANES)) for at in columns]
    rate = jnp.concatenate(rate + rate, axis=0).astype(F32).T.reshape(16, 8, LANES)
    rate = swap(rate, ("l", "z"))
    mine, other = gather_matrices(offsets, x, c)

    out, high, low = pl.pallas_call(
        rows_kernel,
        out_shape=(
            jax.ShapeDtypeStruct((64, 8, LANES), F32),
            jax.ShapeDtypeStruct((2, BLOCK, BLOCK), BF16),
            jax.ShapeDtypeStruct((2, BLOCK, BLOCK), BF16),
        ),
        in_specs=vmem(4),
        out_specs=tuple(vmem(3)),
        compiler_params=PARAMS,
        name="rows",
    )(f, mine, other, row_mask)
    out = swap(out, SPREAD)
    out = pl.pallas_call(
        middle_kernel,
        out_shape=jax.ShapeDtypeStruct((64, 16, LANES), F32),
        in_specs=vmem(3) + [pl.BlockSpec(memory_space=pltpu.SMEM)] + vmem(2),
        out_specs=vmem(1)[0],
        scratch_shapes=[
            pltpu.VMEM((4, 4, 8, BLOCK), F32),
            pltpu.VMEM((2, 8, BLOCK), F32),
        ],
        compiler_params=PARAMS,
        name="middle",
    )(out, rate, col_mask, rate_table, high, low)
    out = swap(out, SPREAD)
    out = pl.pallas_call(
        last_kernel,
        out_shape=jax.ShapeDtypeStruct((2, 2, PIECE, 1024), F32),
        in_specs=vmem(4),
        out_specs=vmem(1)[0],
        compiler_params=PARAMS,
        name="last",
    )(out, row_mask, high, low)
    out = swap(out, "c")
    covariance = jnp.concatenate([out[0, 0], out[1, 0]], axis=1)
    adjoint = jnp.concatenate([out[0, 1], out[1, 1]], axis=1)
    return covariance[None], adjoint[None]


def solution(mesh):
    devices = mesh.devices
    tm, row = devices.shape
    fine = Mesh(devices.reshape(tm // 2, 2, row // 16, 2, 8), ("x", "c", "h", "l", "z"))
    field = P(TIME, ROWS, None)
    return jax.shard_map(
        per_device,
        mesh=fine,
        in_specs=(field, P(ROWS, None), P(), P(), P(), P(None, ROWS, None)),
        out_specs=(field, field),
        check_vma=False,
    )
```

```python
import jax
import jax.numpy as jnp
from jax import lax
from jax.experimental import pallas as pl
from jax.experimental.pallas import tpu as pltpu
from jax.sharding import Mesh
from jax.sharding import PartitionSpec as P

BLOCK = 512
HALF = 256
LANES = 128
PIECE = 32
F32 = jnp.float32
BF16 = jnp.bfloat16
ROWS = ("h", "l", "z")
TIME = ("u", "v", "c")
NEAR = ("u", "l", "z")
SPREAD = ("u", "v", "l", "z")


def split(values):
    high = values.astype(BF16)
    return high, (values - high.astype(F32)).astype(BF16)


def product(both, high, matrix_high, matrix_low, adjoint):
    dims = (((1,), (1 if adjoint else 0,)), ((), ()))
    count = high.shape[0]
    wide = lax.dot_general(both, matrix_high, dims, preferred_element_type=F32)
    small = lax.dot_general(high, matrix_low, dims, preferred_element_type=F32)
    return wide[:count] + (wide[count:] + small)


def by_half(v, own, far):
    return [jnp.where(v == 0, own, far), jnp.where(v == 0, far, own)]


def solve_forward(lines, mask, halves):
    high, low = split(lines)
    both = jnp.concatenate([high, low], axis=0)
    out = []
    for highs, lows in halves:
        parts = [product(both, high, highs[k], lows[k], False) for k in range(2)]
        out.append(jnp.where(mask, parts[0], parts[1]))
    return out


def solve_adjoint(lines, mask, v, halves):
    total = [None, None]
    order = by_half(v, lines[:, :HALF], lines[:, HALF:])
    for piece, (highs, lows) in zip(order, halves):
        high, low = split(piece)
        both = jnp.concatenate([high, low], axis=0)
        for k in range(2):
            part = product(both, high, highs[k], lows[k], True)
            total[k] = part if total[k] is None else total[k] + part
    return lines + jnp.where(mask, total[0], total[1])


def exchange_lanes(tiles):
    group = lax.broadcasted_iota(jnp.int32, tiles[0].shape, 1) // PIECE
    out = []
    for place in range(4):
        made = None
        for source in range(4):
            turn = ((source - place) % 4) * PIECE
            rolled = pltpu.roll(tiles[source], turn, 1) if turn else tiles[source]
            made = rolled if made is None else jnp.where(group == source, rolled, made)
        out.append(made)
    return out


def class_mask(line, first, count, kind, copies):
    lane = lax.broadcasted_iota(jnp.int32, (count, LANES), 1)
    row = lax.broadcasted_iota(jnp.int32, (count, LANES), 0)
    picked = jnp.where((lane == row + first) & (line == kind), 1.0, 0.0)
    return jnp.concatenate([jnp.sum(picked, axis=1, keepdims=True)] * copies, axis=0) > 0.5


def row_mask(class_ref, kind, copies):
    place = lax.axis_index(ROWS)
    line = class_ref[pl.ds(place // 4, 1), :]
    return class_mask(line, lax.rem(place, 4) * PIECE, PIECE, kind, copies)


def rows_kernel(
    f0, f1, f2, f3, mine_ref, other_ref, rate_ref, class_ref, out_ref, high_ref, low_ref
):
    c, v = lax.axis_index("c"), lax.axis_index("v")
    fields = (f0, f1, f2, f3)

    def columns(ref, b, more, width):
        at = pl.multiple_of(c * 1024 + b * BLOCK + more, width)
        return ref[..., pl.ds(at, width)].reshape(PIECE, width)

    lines = jnp.concatenate(
        [columns(f, b, 0, BLOCK) for f in fields for b in range(2)], axis=0
    )
    same = jnp.concatenate(
        [columns(f, b, v * HALF, HALF) for f in fields for b in range(2)], axis=0
    )
    rate = [columns(rate_ref, b, v * HALF, HALF).astype(F32) for b in range(2)]
    rate = jnp.concatenate(rate + rate, axis=0)
    for k, ref in enumerate((mine_ref, other_ref)):
        high, low = split(ref[...])
        high_ref[k] = high
        low_ref[k] = low
    mask = row_mask(class_ref, c, 8)
    solved = solve_forward(lines, mask, [(high_ref, low_ref)])[0] + same
    for n in range(2):
        at = slice(n * LANES, (n + 1) * LANES)
        for place in range(3):
            tile = rate if place == 2 else solved[place * LANES : (place + 1) * LANES]
            out_ref[n * 16 : (n + 1) * 16, place] = tile[:, at].T.reshape(16, 8, LANES)


def middle_kernel(
    x_ref, near_mine, near_other, class_ref, table_ref, high_ref, low_ref,
    out_ref, far_high, far_low, a_ref, r_ref,
):
    c, v, u = lax.axis_index("c"), lax.axis_index("v"), lax.axis_index("u")
    for k, ref in enumerate((near_mine, near_other)):
        high, low = split(ref[...])
        far_high[k] = high
        far_low[k] = low
    tiles = x_ref[...].reshape(2, 4, 4, 3, 8, LANES)
    made = exchange_lanes([tiles[:, :, i, :2].reshape(128, LANES) for i in range(4)])
    for tb in range(4):
        block = made[tb].reshape(2, 4, 2, 8, LANES)
        for q in range(4):
            a_ref[:, :, tb, :, q * LANES : (q + 1) * LANES] = block[:, q]
    made = exchange_lanes([tiles[0, :, i, 2].reshape(32, LANES) for i in range(4)])
    for b in range(2):
        block = made[b].reshape(4, 8, LANES)
        for q in range(4):
            r_ref[b, :, q * LANES : (q + 1) * LANES] = block[q]
    rate = r_ref[...].reshape(16, BLOCK)
    decays = jnp.zeros_like(rate)
    for k in range(16):
        decays = jnp.where(rate == float(k), table_ref[k], decays)
    scaled = jnp.sqrt(1.0 - decays * decays)

    place = lax.axis_index(("l", "z"))
    marks = []
    for b in range(2):
        line = class_ref[pl.ds(c * 8 + b * 4 + v * 2 + u, 1), :]
        marks.append(class_mask(line, place * 8, 8, c, 1).astype(F32))
    mask = jnp.concatenate(marks * 8, axis=0) > 0.5
    halves = [(high_ref, low_ref), (far_high, far_low)]
    lines = a_ref[...].reshape(128, BLOCK)
    solved = by_half(v, *solve_forward(lines, mask, halves))
    smoothed = (lines + jnp.concatenate(solved, axis=1)).reshape(2, 2, 2, 16, BLOCK)
    state, field = None, []
    for t in range(8):
        far, late, core = t // 4, (t // 2) % 2, t % 2
        pair = smoothed[far]
        pair = jnp.where(v == 0, pair[late], pair[1 - late])
        here = scaled * jnp.where(c == 0, pair[core], pair[1 - core])
        state = here if state is None else decays * state + here
        field.append(state)
    state, back = None, [None] * 8
    for t in range(7, -1, -1):
        here = scaled * field[t]
        state = here if state is None else decays * state + here
        back[t] = state
    adjoint = solve_adjoint(jnp.concatenate(back, axis=0), mask, v, halves)
    field = jnp.concatenate(field, axis=0)
    for n, value in enumerate((field, adjoint)):
        parts = value.reshape(4, 4, 8, BLOCK)
        for q in range(4):
            tiles = [
                parts[:, tb, :, q * LANES : (q + 1) * LANES].reshape(32, LANES)
                for tb in range(4)
            ]
            made = exchange_lanes(tiles)
            for i in range(4):
                block = made[i].reshape(4, 8, LANES)
                for x in range(4):
                    out_ref[x * 16 + q * 4 + i, n * 8 : (n + 1) * 8, :] = block[x]


def last_kernel(
    x_ref, class_ref, high_ref, low_ref, far_high, far_low, out_ref
):
    c, v = lax.axis_index("c"), lax.axis_index("v")
    pieces = [[], []]
    for s in range(4):
        x = (s % 2) * 2 + s // 2
        for n in range(2):
            tile = x_ref[x * 16 : (x + 1) * 16, n * 8 : (n + 1) * 8, :]
            pieces[n].append(tile.reshape(LANES, LANES).T)
    field = jnp.concatenate(pieces[0], axis=1)
    lines = jnp.concatenate(pieces[1], axis=1)
    mask = row_mask(class_ref, c, 4)
    halves = [(high_ref, low_ref), (far_high, far_low)]
    solved = solve_adjoint(lines, mask, v, halves)
    for n, value in enumerate((field, solved)):
        for t in range(2):
            for b in range(2):
                first = (t * 2 + b) * PIECE
                out_ref[t, n, :, b * BLOCK : (b + 1) * BLOCK] = value[
                    first : first + PIECE
                ]


def vmem(count):
    return [pl.BlockSpec(memory_space=pltpu.VMEM)] * count


PARAMS = pltpu.CompilerParams(vmem_limit_bytes=40 * 1024 * 1024)
HALVES = (jax.ShapeDtypeStruct((2, BLOCK, HALF), BF16),) * 2


def swap(values, axis):
    return lax.all_to_all(values, axis, split_axis=0, concat_axis=0, tiled=True)


def to_partners(values):
    core = lax.ppermute(values, "c", [(0, 1), (1, 0)])
    near = lax.ppermute(values, "v", [(0, 1), (1, 0)])
    both = lax.ppermute(values, ("v", "c"), [(k, 3 - k) for k in range(4)])
    return core, near, both


def per_device(forcing, rate_class, rate_table, row_class, col_class, offsets):
    c, v = lax.axis_index("c"), lax.axis_index("v")
    row_lines = row_class.reshape(-1, LANES)
    col_lines = col_class.reshape(-1, LANES)

    fields = (forcing,) + to_partners(forcing)
    rows = offsets.shape[1]
    piece = lax.dynamic_slice(offsets, (c, 0, v * HALF), (1, rows, HALF))
    pieces = jnp.broadcast_to(piece, (BLOCK // rows, rows, HALF))
    mine = swap(pieces, ROWS).reshape(BLOCK, HALF)
    mine, *fields = lax.optimization_barrier((mine,) + fields)
    other, near_mine, near_other = to_partners(mine)

    out, high, low = pl.pallas_call(
        rows_kernel,
        out_shape=(jax.ShapeDtypeStruct((32, 3, 8, LANES), F32),) + HALVES,
        in_specs=vmem(8),
        out_specs=tuple(vmem(3)),
        compiler_params=PARAMS,
        name="rows",
    )(*fields, mine, other, rate_class, row_lines)
    out = swap(out, NEAR)
    out, far_high, far_low = pl.pallas_call(
        middle_kernel,
        out_shape=(jax.ShapeDtypeStruct((64, 16, LANES), F32),) + HALVES,
        in_specs=vmem(4) + [pl.BlockSpec(memory_space=pltpu.SMEM)] + vmem(2),
        out_specs=tuple(vmem(3)),
        scratch_shapes=[
            pltpu.VMEM((2, 2, 4, 8, BLOCK), F32),
            pltpu.VMEM((2, 8, BLOCK), F32),
        ],
        compiler_params=PARAMS,
        name="middle",
    )(out, near_mine, near_other, col_lines, rate_table, high, low)
    out = swap(out, SPREAD)
    out = pl.pallas_call(
        last_kernel,
        out_shape=jax.ShapeDtypeStruct((2, 2, PIECE, 1024), F32),
        in_specs=vmem(6),
        out_specs=vmem(1)[0],
        compiler_params=PARAMS,
        name="last",
    )(out, row_lines, high, low, far_high, far_low)
    out = swap(out, "c")
    covariance = jnp.concatenate([out[0, 0], out[1, 0]], axis=1)
    adjoint = jnp.concatenate([out[0, 1], out[1, 1]], axis=1)
    return covariance[None], adjoint[None]


def solution(mesh):
    devices = mesh.devices
    tm, row = devices.shape
    fine = Mesh(
        devices.reshape(tm // 4, 2, 2, row // 16, 2, 8), ("u", "v", "c", "h", "l", "z")
    )
    field = P(TIME, ROWS, None)
    return jax.shard_map(
        per_device,
        mesh=fine,
        in_specs=(field, P(ROWS, None), P(), P(), P(), P(None, ROWS, None)),
        out_specs=(field, field),
        check_vma=False,
    )
```

```python
import jax
import jax.numpy as jnp
from jax import lax
from jax.experimental import pallas as pl
from jax.experimental.pallas import tpu as pltpu
from jax.sharding import Mesh
from jax.sharding import PartitionSpec as P

BLOCK = 512
HALF = 256
LANES = 128
PIECE = 32
F32 = jnp.float32
BF16 = jnp.bfloat16
ROWS = ("h", "l", "z")
TIME = ("u", "v", "c")
NEAR = ("u", "l", "z")
SPREAD = ("u", "v", "l", "z")


def split(values):
    high = values.astype(BF16)
    return high, (values - high.astype(F32)).astype(BF16)


def product(both, high, matrix_high, matrix_low, adjoint):
    dims = (((1,), (1 if adjoint else 0,)), ((), ()))
    count = high.shape[0]
    wide = lax.dot_general(both, matrix_high, dims, preferred_element_type=F32)
    small = lax.dot_general(high, matrix_low, dims, preferred_element_type=F32)
    return wide[:count] + (wide[count:] + small)


def by_half(v, own, far):
    return [jnp.where(v == 0, own, far), jnp.where(v == 0, far, own)]


def solve_forward(lines, mask, halves):
    high, low = split(lines)
    both = jnp.concatenate([high, low], axis=0)
    out = []
    for highs, lows in halves:
        parts = [product(both, high, highs[k], lows[k], False) for k in range(2)]
        out.append(jnp.where(mask, parts[0], parts[1]))
    return out


def solve_adjoint(lines, mask, v, halves):
    total = [None, None]
    order = by_half(v, lines[:, :HALF], lines[:, HALF:])
    for piece, (highs, lows) in zip(order, halves):
        high, low = split(piece)
        both = jnp.concatenate([high, low], axis=0)
        for k in range(2):
            part = product(both, high, highs[k], lows[k], True)
            total[k] = part if total[k] is None else total[k] + part
    return lines + jnp.where(mask, total[0], total[1])


def exchange_lanes(tiles):
    group = lax.broadcasted_iota(jnp.int32, tiles[0].shape, 1) // PIECE
    out = []
    for place in range(4):
        made = None
        for source in range(4):
            turn = ((source - place) % 4) * PIECE
            rolled = pltpu.roll(tiles[source], turn, 1) if turn else tiles[source]
            made = rolled if made is None else jnp.where(group == source, rolled, made)
        out.append(made)
    return out


def class_mask(line, first, count, kind, copies):
    lane = lax.broadcasted_iota(jnp.int32, (count, LANES), 1)
    row = lax.broadcasted_iota(jnp.int32, (count, LANES), 0)
    picked = jnp.where((lane == row + first) & (line == kind), 1.0, 0.0)
    return jnp.concatenate([jnp.sum(picked, axis=1, keepdims=True)] * copies, axis=0) > 0.5


def row_mask(class_ref, kind, copies):
    place = lax.axis_index(ROWS)
    line = class_ref[pl.ds(place // 4, 1), :]
    return class_mask(line, lax.rem(place, 4) * PIECE, PIECE, kind, copies)


def rows_kernel(
    f0, f1, f2, f3, mine_ref, other_ref, rate_ref, class_ref, table_ref,
    out_ref, high_ref, low_ref,
):
    c, v = lax.axis_index("c"), lax.axis_index("v")
    fields = (f0, f1, f2, f3)

    def columns(ref, at, width):
        at = pl.multiple_of(at, width)
        return ref[..., pl.ds(at, width)].reshape(PIECE, width)

    lines = jnp.concatenate(
        [columns(f, b * BLOCK, BLOCK) for f in fields for b in range(2)], axis=0
    )
    at = [b * BLOCK + v * HALF for b in range(2)]
    same = jnp.concatenate([columns(f, a, HALF) for f in fields for a in at], axis=0)
    rate = [columns(rate_ref, c * 1024 + a, HALF) for a in at]
    rate = jnp.concatenate(rate, axis=0)
    decays = jnp.zeros(rate.shape, F32)
    for k in range(16):
        decays = jnp.where(rate == k, table_ref[k], decays)
    decays = jnp.concatenate([decays, decays], axis=0)
    for k, ref in enumerate((mine_ref, other_ref)):
        high, low = split(ref[...])
        high_ref[k] = high
        low_ref[k] = low
    mask = row_mask(class_ref, c, 8)
    solved = solve_forward(lines, mask, [(high_ref, low_ref)])[0] + same
    for n in range(2):
        at = slice(n * LANES, (n + 1) * LANES)
        for place in range(3):
            tile = decays if place == 2 else solved[place * LANES : (place + 1) * LANES]
            out_ref[n * 16 : (n + 1) * 16, place] = tile[:, at].T.reshape(16, 8, LANES)


def middle_kernel(
    x_ref, near_mine, near_other, class_ref, high_ref, low_ref,
    out_ref, far_high, far_low, a_ref, r_ref,
):
    c, v, u = lax.axis_index("c"), lax.axis_index("v"), lax.axis_index("u")
    for k, ref in enumerate((near_mine, near_other)):
        high, low = split(ref[...])
        far_high[k] = high
        far_low[k] = low
    tiles = x_ref[...].reshape(2, 4, 4, 3, 8, LANES)
    made = exchange_lanes([tiles[:, :, i, :2].reshape(128, LANES) for i in range(4)])
    for tb in range(4):
        block = made[tb].reshape(2, 4, 2, 8, LANES)
        for q in range(4):
            a_ref[:, :, tb, :, q * LANES : (q + 1) * LANES] = block[:, q]
    made = exchange_lanes([tiles[0, :, i, 2].reshape(32, LANES) for i in range(4)])
    for b in range(2):
        block = made[b].reshape(4, 8, LANES)
        for q in range(4):
            r_ref[b, :, q * LANES : (q + 1) * LANES] = block[q]
    decays = r_ref[...].reshape(16, BLOCK)
    scaled = jnp.sqrt(1.0 - decays * decays)

    place = lax.axis_index(("l", "z"))
    marks = []
    for b in range(2):
        line = class_ref[pl.ds(c * 8 + b * 4 + v * 2 + u, 1), :]
        marks.append(class_mask(line, place * 8, 8, c, 1).astype(F32))
    mask = jnp.concatenate(marks * 8, axis=0) > 0.5
    halves = [(high_ref, low_ref), (far_high, far_low)]
    lines = a_ref[...].reshape(128, BLOCK)
    solved = by_half(v, *solve_forward(lines, mask, halves))
    smoothed = (lines + jnp.concatenate(solved, axis=1)).reshape(2, 2, 2, 16, BLOCK)
    state, field = None, []
    for t in range(8):
        far, late, core = t // 4, (t // 2) % 2, t % 2
        pair = smoothed[far]
        pair = jnp.where(v == 0, pair[late], pair[1 - late])
        here = scaled * jnp.where(c == 0, pair[core], pair[1 - core])
        state = here if state is None else decays * state + here
        field.append(state)
    state, back = None, [None] * 8
    for t in range(7, -1, -1):
        here = scaled * field[t]
        state = here if state is None else decays * state + here
        back[t] = state
    adjoint = solve_adjoint(jnp.concatenate(back, axis=0), mask, v, halves)
    field = jnp.concatenate(field, axis=0)
    for n, value in enumerate((field, adjoint)):
        parts = value.reshape(4, 4, 8, BLOCK)
        for q in range(4):
            tiles = [
                parts[:, tb, :, q * LANES : (q + 1) * LANES].reshape(32, LANES)
                for tb in range(4)
            ]
            made = exchange_lanes(tiles)
            for i in range(4):
                block = made[i].reshape(4, 8, LANES)
                for x in range(4):
                    out_ref[x * 16 + q * 4 + i, n * 8 : (n + 1) * 8, :] = block[x]


def last_kernel(
    x_ref, class_ref, high_ref, low_ref, far_high, far_low, keep_ref, send_ref
):
    c, v = lax.axis_index("c"), lax.axis_index("v")
    pieces = [[], []]
    for s in range(4):
        x = (s % 2) * 2 + s // 2
        for n in range(2):
            tile = x_ref[x * 16 : (x + 1) * 16, n * 8 : (n + 1) * 8, :]
            pieces[n].append(tile.reshape(LANES, LANES).T)
    field = jnp.concatenate(pieces[0], axis=1)
    lines = jnp.concatenate(pieces[1], axis=1)
    mask = row_mask(class_ref, c, 4)
    halves = [(high_ref, low_ref), (far_high, far_low)]
    solved = solve_adjoint(lines, mask, v, halves)
    for n, value in enumerate((field, solved)):
        times = value[: 2 * PIECE], value[2 * PIECE :]
        for ref, first in ((keep_ref, 0), (send_ref, 1)):
            chosen = jnp.where(c == first, times[0], times[1])
            for b in range(2):
                lines = chosen[b * PIECE : (b + 1) * PIECE]
                ref[n, :, b * BLOCK : (b + 1) * BLOCK] = lines


def join_kernel(keep_ref, got_ref, field_ref, adjoint_ref):
    c = lax.axis_index("c")
    for n, ref in enumerate((field_ref, adjoint_ref)):
        for part, place in ((keep_ref, c), (got_ref, 1 - c)):
            ref[0, :, pl.ds(pl.multiple_of(place * 1024, 1024), 1024)] = part[n]


def vmem(count):
    return [pl.BlockSpec(memory_space=pltpu.VMEM)] * count


PARAMS = pltpu.CompilerParams(vmem_limit_bytes=40 * 1024 * 1024)
HALVES = (jax.ShapeDtypeStruct((2, BLOCK, HALF), BF16),) * 2


def swap(values, axis):
    return lax.all_to_all(values, axis, split_axis=0, concat_axis=0, tiled=True)


CORE = [(0, 1), (1, 0)]
BOTH = [(k, 3 - k) for k in range(4)]


def per_device(forcing, rate_class, rate_table, row_class, col_class, offsets):
    c, v = lax.axis_index("c"), lax.axis_index("v")
    row_lines = row_class.reshape(-1, LANES)
    col_lines = col_class.reshape(-1, LANES)

    rows = offsets.shape[1]
    piece = lax.dynamic_slice(offsets, (c, 0, v * HALF), (1, rows, HALF))
    pieces = jnp.broadcast_to(piece, (BLOCK // rows, rows, HALF))
    mine = swap(pieces, ROWS).reshape(BLOCK, HALF)

    field = lax.dynamic_slice(forcing[0], (0, c * 1024), (PIECE, 1024))
    cross = lax.dynamic_slice(forcing[0], (0, (1 - c) * 1024), (PIECE, 1024))
    fields = (
        field,
        lax.ppermute(cross, "c", CORE),
        lax.ppermute(field, "v", CORE),
        lax.ppermute(cross, ("v", "c"), BOTH),
    )
    mine, *fields = lax.optimization_barrier((mine,) + fields)
    other = lax.ppermute(mine, "c", CORE)
    near_mine = lax.ppermute(mine, "v", CORE)
    near_other = lax.ppermute(near_mine, "c", CORE)

    smem = pl.BlockSpec(memory_space=pltpu.SMEM)
    out, high, low = pl.pallas_call(
        rows_kernel,
        out_shape=(jax.ShapeDtypeStruct((32, 3, 8, LANES), F32),) + HALVES,
        in_specs=vmem(8) + [smem],
        out_specs=tuple(vmem(3)),
        compiler_params=PARAMS,
        name="rows",
    )(*fields, mine, other, rate_class, row_lines, rate_table)
    out = swap(out, NEAR)
    out, near_mine, near_other = lax.optimization_barrier((out, near_mine, near_other))
    out, far_high, far_low = pl.pallas_call(
        middle_kernel,
        out_shape=(jax.ShapeDtypeStruct((64, 16, LANES), F32),) + HALVES,
        in_specs=vmem(6),
        out_specs=tuple(vmem(3)),
        scratch_shapes=[
            pltpu.VMEM((2, 2, 4, 8, BLOCK), F32),
            pltpu.VMEM((2, 8, BLOCK), F32),
        ],
        compiler_params=PARAMS,
        name="middle",
    )(out, near_mine, near_other, col_lines, high, low)
    out = swap(out, SPREAD)
    keep, send = pl.pallas_call(
        last_kernel,
        out_shape=(jax.ShapeDtypeStruct((2, PIECE, 1024), F32),) * 2,
        in_specs=vmem(6),
        out_specs=tuple(vmem(2)),
        compiler_params=PARAMS,
        name="last",
    )(out, row_lines, high, low, far_high, far_low)
    got = lax.ppermute(send, "c", CORE)
    return pl.pallas_call(
        join_kernel,
        out_shape=(jax.ShapeDtypeStruct(forcing.shape, F32),) * 2,
        in_specs=vmem(2),
        out_specs=tuple(vmem(2)),
        compiler_params=PARAMS,
        name="join",
    )(keep, got)


def solution(mesh):
    devices = mesh.devices
    tm, row = devices.shape
    fine = Mesh(
        devices.reshape(tm // 4, 2, 2, row // 16, 2, 8), ("u", "v", "c", "h", "l", "z")
    )
    field = P(TIME, ROWS, None)
    return jax.shard_map(
        per_device,
        mesh=fine,
        in_specs=(field, P(ROWS, None), P(), P(), P(), P(None, ROWS, None)),
        out_specs=(field, field),
        check_vma=False,
    )
```

```python
import jax
import jax.numpy as jnp
from jax import lax
from jax.experimental import pallas as pl
from jax.experimental.pallas import tpu as pltpu
from jax.sharding import Mesh
from jax.sharding import PartitionSpec as P

BLOCK = 512
LANES = 128
PIECE = 32
F32 = jnp.float32
BF16 = jnp.bfloat16
ROWS = ("h", "l", "z")
TIME = ("u", "v", "c")
NEAR = ("u", "l", "z")
SPREAD = ("u", "v", "c", "l", "z")


def split(values):
    high = values.astype(BF16)
    return high, (values - high.astype(F32)).astype(BF16)


def product(both, high, low, adjoint):
    dims = (((1,), (1 if adjoint else 0,)), ((), ()))
    count = both.shape[0] // 2
    wide = lax.dot_general(both, high, dims, preferred_element_type=F32)
    small = lax.dot_general(both[:count], low, dims, preferred_element_type=F32)
    return wide[:count] + (wide[count:] + small)


def own_first(lines, v, c):
    quarters = [lines[:, k * LANES : (k + 1) * LANES] for k in range(4)]
    quarters = [jnp.where(v == 0, quarters[k], quarters[(k + 2) % 4]) for k in range(4)]
    quarters = [jnp.where(c == 0, quarters[k], quarters[k ^ 1]) for k in range(4)]
    return jnp.concatenate(quarters, axis=1)


def matrix(own_ref, rest_ref, k):
    return jnp.concatenate([own_ref[:, k * LANES : (k + 1) * LANES], rest_ref[k]], axis=1)


def solve(lines, mask, matrices, adjoint):
    own_high, own_low, rest_high, rest_low = matrices
    both = jnp.concatenate(split(lines), axis=0)
    parts = []
    for k in range(2):
        high, low = matrix(own_high, rest_high, k), matrix(own_low, rest_low, k)
        parts.append(product(both, high, low, adjoint))
    return jnp.where(mask, parts[0], parts[1])


def exchange_lanes(tiles):
    group = lax.broadcasted_iota(jnp.int32, tiles[0].shape, 1) // PIECE
    out = []
    for place in range(4):
        made = None
        for source in range(4):
            turn = ((source - place) % 4) * PIECE
            rolled = pltpu.roll(tiles[source], turn, 1) if turn else tiles[source]
            made = rolled if made is None else jnp.where(group == source, rolled, made)
        out.append(made)
    return out


def class_marks(line, first, count):
    lane = lax.broadcasted_iota(jnp.int32, (count, LANES), 1)
    row = lax.broadcasted_iota(jnp.int32, (count, LANES), 0)
    picked = jnp.where((lane == row + first) & (line == 0), 1.0, 0.0)
    return jnp.sum(picked, axis=1, keepdims=True)


def row_mask(class_ref, copies):
    place = lax.axis_index(ROWS)
    line = class_ref[pl.ds(place // 4, 1), :]
    marks = class_marks(line, lax.rem(place, 4) * PIECE, PIECE)
    return jnp.concatenate([marks] * copies, axis=0) > 0.5


def lines_kernel(f0, f1, f2, f3, rate_ref, table_ref, both_ref, same_ref, decays_ref):
    quarter = lax.axis_index("v") * 2 + lax.axis_index("c")
    fields = ((f0, f1), (f2, f3))
    at = [pl.multiple_of(b * BLOCK + quarter * LANES, LANES) for b in range(4)]
    for far in range(2):
        for pair in range(2):
            for core in range(2):
                for b in range(2):
                    ref, block = fields[far][core], pair * 2 + b
                    first = (((far * 2 + pair) * 2 + core) * 2 + b) * PIECE
                    rows = pl.ds(first, PIECE)
                    lines = ref[0, :, block * BLOCK : (block + 1) * BLOCK]
                    high, low = split(lines)
                    both_ref[rows, :] = high
                    both_ref[pl.ds(512 + first, PIECE), :] = low
                    same_ref[rows, :] = ref[0, :, pl.ds(at[block], LANES)]
    for pair in range(2):
        rate = [rate_ref[:, pl.ds(at[pair * 2 + b], LANES)] for b in range(2)]
        rate = jnp.concatenate(rate, axis=0)
        decays = jnp.zeros(rate.shape, F32)
        for k in range(16):
            decays = jnp.where(rate == k, table_ref[k], decays)
        decays = jnp.concatenate([decays, decays], axis=0).T.reshape(16, 8, LANES)
        decays_ref[pair * 16 : (pair + 1) * 16] = decays


def rows_kernel(
    both_ref, same_ref, decays_ref, m_ref, class_ref, out_ref, high_ref, low_ref
):
    for k in range(2):
        high, low = split(m_ref[:, k].reshape(BLOCK, LANES))
        high_ref[:, k * LANES : (k + 1) * LANES] = high
        low_ref[:, k * LANES : (k + 1) * LANES] = low
    solved = product(both_ref[...], high_ref[...], low_ref[...], False)
    solved = jnp.where(row_mask(class_ref, 16), solved[:, :LANES], solved[:, LANES:])
    solved = solved + same_ref[...]
    for pair in range(2):
        at = slice(pair * 16, (pair + 1) * 16)
        for far in range(2):
            first = (far * 2 + pair) * LANES
            turned = solved[first : first + LANES].T
            out_ref[at, far] = turned.reshape(16, 8, LANES)
        out_ref[at, 2] = decays_ref[at]


def rest_kernel(m1, m2, m3, high_ref, low_ref):
    for n, ref in enumerate((m1, m2, m3)):
        for k in range(2):
            high, low = split(ref[:, k].reshape(BLOCK, LANES))
            high_ref[k, :, n * LANES : (n + 1) * LANES] = high
            low_ref[k, :, n * LANES : (n + 1) * LANES] = low


def middle_kernel(x_ref, class_ref, h0, l0, h1, l1, out_ref, a_ref, r_ref):
    c, v, u = lax.axis_index("c"), lax.axis_index("v"), lax.axis_index("u")
    tiles = x_ref[...].reshape(2, 4, 4, 3, 8, LANES)
    made = exchange_lanes([tiles[:, :, i, :2].reshape(128, LANES) for i in range(4)])
    for tb in range(4):
        block = made[tb].reshape(2, 4, 2, 8, LANES)
        for q in range(4):
            a_ref[:, :, tb, :, q * LANES : (q + 1) * LANES] = block[:, q]
    made = exchange_lanes([tiles[0, :, i, 2].reshape(32, LANES) for i in range(4)])
    for b in range(2):
        block = made[b].reshape(4, 8, LANES)
        for q in range(4):
            r_ref[b, :, q * LANES : (q + 1) * LANES] = block[q]
    decays = r_ref[...].reshape(16, BLOCK)
    scaled = jnp.sqrt(1.0 - decays * decays)

    place = lax.axis_index(("l", "z"))
    marks = []
    for b in range(2):
        line = class_ref[pl.ds((u * 2 + b) * 4 + v * 2 + c, 1), :]
        marks.append(class_marks(line, place * 8, 8))
    mask = jnp.concatenate(marks * 8, axis=0) > 0.5
    matrices = (h0, l0, h1, l1)
    lines = a_ref[...].reshape(128, BLOCK)
    smoothed = lines + own_first(solve(lines, mask, matrices, False), v, c)
    smoothed = smoothed.reshape(2, 2, 2, 16, BLOCK)
    state, field = None, []
    for t in range(8):
        far, late, core = t // 4, (t // 2) % 2, t % 2
        pair = smoothed[far]
        pair = jnp.where(v == 0, pair[late], pair[1 - late])
        here = scaled * jnp.where(c == 0, pair[core], pair[1 - core])
        state = here if state is None else decays * state + here
        field.append(state)
    state, back = None, [None] * 8
    for t in range(7, -1, -1):
        here = scaled * field[t]
        state = here if state is None else decays * state + here
        back[t] = state
    back = jnp.concatenate(back, axis=0)
    adjoint = back + solve(own_first(back, v, c), mask, matrices, True)
    field = jnp.concatenate(field, axis=0).reshape(4, 4, 8, BLOCK)
    adjoint = adjoint.reshape(4, 4, 8, BLOCK)
    for core in range(2):
        for q in range(4):
            lanes = slice(q * LANES, (q + 1) * LANES)
            tiles = [
                value[:, core * 2 + b, :, lanes].reshape(32, LANES)
                for value in (field, adjoint)
                for b in range(2)
            ]
            made = exchange_lanes(tiles)
            for i in range(4):
                block = made[i].reshape(4, 8, LANES)
                for x in range(4):
                    out_ref[(x * 2 + core) * 16 + q * 4 + i] = block[x]


def last_kernel(x_ref, class_ref, h0, l0, h1, l1, field_ref, adjoint_ref):
    c, v = lax.axis_index("c"), lax.axis_index("v")
    lines = []
    for u in range(2):
        pieces = []
        for k in range(4):
            first = (u * 4 + k) * 16
            turned = x_ref[first : first + 16].reshape(LANES, LANES).T
            for b in range(2):
                at = (u * 2 + b) * BLOCK + k * LANES
                field_ref[0, :, at : at + LANES] = turned[b * PIECE : (b + 1) * PIECE]
            pieces.append(turned[2 * PIECE :])
        lines.append(jnp.concatenate(pieces, axis=1))
    lines = jnp.concatenate(lines, axis=0)
    mask = row_mask(class_ref, 4)
    solved = lines + solve(own_first(lines, v, c), mask, (h0, l0, h1, l1), True)
    for b in range(4):
        piece = solved[b * PIECE : (b + 1) * PIECE]
        adjoint_ref[0, :, b * BLOCK : (b + 1) * BLOCK] = piece


def call(kernel, name, shapes, operands, smem=(), scratch=()):
    vmem = pl.BlockSpec(memory_space=pltpu.VMEM)
    places = [
        pl.BlockSpec(memory_space=pltpu.SMEM) if k in smem else vmem
        for k in range(len(operands))
    ]
    return pl.pallas_call(
        kernel,
        out_shape=tuple(jax.ShapeDtypeStruct(*shape) for shape in shapes),
        in_specs=places,
        out_specs=(vmem,) * len(shapes),
        scratch_shapes=[pltpu.VMEM(shape, F32) for shape in scratch],
        compiler_params=pltpu.CompilerParams(vmem_limit_bytes=40 * 1024 * 1024),
        name=name,
    )(*operands)


def swap(values, axis):
    return lax.all_to_all(values, axis, split_axis=0, concat_axis=0, tiled=True)


def partners(values):
    other = [(0, 1), (1, 0)]
    near = lax.ppermute(values, "v", other)
    core = lax.ppermute(values, "c", other)
    return core, near, lax.ppermute(near, "c", other)


def per_device(forcing, rate_class, rate_table, row_class, col_class, offsets):
    row_lines = row_class.reshape(-1, LANES)
    col_lines = col_class.reshape(-1, LANES)

    quarter = lax.axis_index("v") * 2 + lax.axis_index("c")
    rows = offsets.shape[1]
    piece = lax.dynamic_slice(offsets, (0, 0, quarter * LANES), (2, rows, LANES))
    piece = piece.reshape(2 * rows, LANES)
    own = swap(jnp.broadcast_to(piece, (BLOCK // rows, 2 * rows, LANES)), ROWS)

    shapes = (((1024, BLOCK), BF16), ((512, LANES), F32), ((32, 8, LANES), F32))
    operands = (forcing,) + partners(forcing) + (rate_class, rate_table)
    lines = call(lines_kernel, "lines", shapes, operands, smem=(5,))
    own, *lines = lax.optimization_barrier((own,) + lines)
    own = own.reshape(-1, 2, rows, LANES)
    rest = partners(own)

    shapes = (((32, 3, 8, LANES), F32),) + (((BLOCK, 256), BF16),) * 2
    operands = (*lines, own, row_lines)
    out, *own = call(rows_kernel, "rows", shapes, operands)
    out = swap(out, NEAR)
    shapes = (((2, BLOCK, 384), BF16),) * 2
    rest = call(rest_kernel, "rest", shapes, rest)
    out, *rest = lax.optimization_barrier((out,) + rest)
    matrices = (*own, *rest)
    (out,) = call(
        middle_kernel,
        "middle",
        (((128, 8, LANES), F32),),
        (out, col_lines) + matrices,
        scratch=((2, 2, 4, 8, BLOCK), (2, 8, BLOCK)),
    )
    out = swap(out, SPREAD)
    shapes = ((forcing.shape, F32),) * 2
    return call(last_kernel, "last", shapes, (out, row_lines) + matrices)


def solution(mesh):
    devices = mesh.devices
    tm, row = devices.shape
    fine = Mesh(
        devices.reshape(tm // 4, 2, 2, row // 16, 2, 8), ("u", "v", "c", "h", "l", "z")
    )
    field = P(TIME, ROWS, None)
    return jax.shard_map(
        per_device,
        mesh=fine,
        in_specs=(field, P(ROWS, None), P(), P(), P(), P(None, ROWS, None)),
        out_specs=(field, field),
        check_vma=False,
    )
```

```python
import jax
import jax.numpy as jnp
from jax import lax
from jax.experimental import pallas as pl
from jax.experimental.pallas import tpu as pltpu
from jax.sharding import Mesh
from jax.sharding import PartitionSpec as P

BLOCK = 512
LANES = 128
PIECE = 32
F32 = jnp.float32
BF16 = jnp.bfloat16
ROWS = ("h", "l", "z")
TIME = ("u", "v", "c")
NEAR = ("u", "l", "z")
SPREAD = ("l", "z", "u", "v", "c")


def split(values):
    high = values.astype(BF16)
    return high, (values - high.astype(F32)).astype(BF16)


def product(both, high, low, adjoint):
    dims = (((1,), (1 if adjoint else 0,)), ((), ()))
    count = both.shape[0] // 2
    wide = lax.dot_general(both, high, dims, preferred_element_type=F32)
    small = lax.dot_general(both[:count], low, dims, preferred_element_type=F32)
    return wide[:count] + (wide[count:] + small)


def own_first(lines, v, c):
    quarters = [lines[:, k * LANES : (k + 1) * LANES] for k in range(4)]
    quarters = [jnp.where(v == 0, quarters[k], quarters[(k + 2) % 4]) for k in range(4)]
    quarters = [jnp.where(c == 0, quarters[k], quarters[k ^ 1]) for k in range(4)]
    return jnp.concatenate(quarters, axis=1)


def matrix(own_ref, rest_ref, k):
    return jnp.concatenate([own_ref[:, k * LANES : (k + 1) * LANES], rest_ref[k]], axis=1)


def solve(lines, mask, matrices, adjoint):
    own_high, own_low, rest_high, rest_low = matrices
    both = jnp.concatenate(split(lines), axis=0)
    parts = []
    for k in range(2):
        high, low = matrix(own_high, rest_high, k), matrix(own_low, rest_low, k)
        parts.append(product(both, high, low, adjoint))
    return jnp.where(mask, parts[0], parts[1])


def exchange_lanes(tiles):
    group = lax.broadcasted_iota(jnp.int32, tiles[0].shape, 1) // PIECE
    out = []
    for place in range(4):
        made = None
        for source in range(4):
            turn = ((source - place) % 4) * PIECE
            rolled = pltpu.roll(tiles[source], turn, 1) if turn else tiles[source]
            made = rolled if made is None else jnp.where(group == source, rolled, made)
        out.append(made)
    return out


def class_marks(line, first, count):
    lane = lax.broadcasted_iota(jnp.int32, (count, LANES), 1)
    row = lax.broadcasted_iota(jnp.int32, (count, LANES), 0)
    picked = jnp.where((lane == row + first) & (line == 0), 1.0, 0.0)
    return jnp.sum(picked, axis=1, keepdims=True)


def row_mask(class_ref, copies):
    place = lax.axis_index(ROWS)
    line = class_ref[pl.ds(place // 4, 1), :]
    marks = class_marks(line, lax.rem(place, 4) * PIECE, PIECE)
    return jnp.concatenate([marks] * copies, axis=0) > 0.5


def lines_kernel(f0, f1, f2, f3, rate_ref, table_ref, both_ref, same_ref, decays_ref):
    quarter = lax.axis_index("v") * 2 + lax.axis_index("c")
    fields = ((f0, f1), (f2, f3))
    at = [pl.multiple_of(b * BLOCK + quarter * LANES, LANES) for b in range(4)]
    for far in range(2):
        for pair in range(2):
            for core in range(2):
                for b in range(2):
                    ref, block = fields[far][core], pair * 2 + b
                    first = (((far * 2 + pair) * 2 + core) * 2 + b) * PIECE
                    rows = pl.ds(first, PIECE)
                    lines = ref[0, :, block * BLOCK : (block + 1) * BLOCK]
                    high, low = split(lines)
                    both_ref[rows, :] = high
                    both_ref[pl.ds(512 + first, PIECE), :] = low
                    same_ref[rows, :] = ref[0, :, pl.ds(at[block], LANES)]
    for pair in range(2):
        rate = [rate_ref[:, pl.ds(at[pair * 2 + b], LANES)] for b in range(2)]
        rate = jnp.concatenate(rate, axis=0)
        decays = jnp.zeros(rate.shape, F32)
        for k in range(16):
            decays = jnp.where(rate == k, table_ref[k], decays)
        decays = jnp.concatenate([decays, decays], axis=0).T.reshape(16, 8, LANES)
        decays_ref[pair * 16 : (pair + 1) * 16] = decays


def rows_kernel(
    both_ref, same_ref, decays_ref, m_ref, class_ref,
    out_ref, high_ref, low_ref, first_ref, second_ref,
):
    half = m_ref.shape[0] // 2
    first_ref[...] = m_ref[:half]
    second_ref[...] = m_ref[half:]
    for k in range(2):
        high, low = split(m_ref[:, k].reshape(BLOCK, LANES))
        high_ref[:, k * LANES : (k + 1) * LANES] = high
        low_ref[:, k * LANES : (k + 1) * LANES] = low
    solved = product(both_ref[...], high_ref[...], low_ref[...], False)
    solved = jnp.where(row_mask(class_ref, 16), solved[:, :LANES], solved[:, LANES:])
    solved = solved + same_ref[...]
    for pair in range(2):
        at = slice(pair * 16, (pair + 1) * 16)
        for far in range(2):
            first = (far * 2 + pair) * LANES
            turned = solved[first : first + LANES].T
            out_ref[at, far] = turned.reshape(16, 8, LANES)
        out_ref[at, 2] = decays_ref[at]


def rest_kernel(m1, near1, near2, both1, both2, high_ref, low_ref):
    for n, refs in enumerate(((m1,), (near1, near2), (both1, both2))):
        lanes = slice(n * LANES, (n + 1) * LANES)
        count = BLOCK // len(refs)
        for k in range(2):
            for part, ref in enumerate(refs):
                rows = slice(part * count, (part + 1) * count)
                high, low = split(ref[:, k].reshape(count, LANES))
                high_ref[k, rows, lanes] = high
                low_ref[k, rows, lanes] = low


def middle_kernel(x_ref, class_ref, h0, l0, h1, l1, out_ref, a_ref, r_ref):
    c, v, u = lax.axis_index("c"), lax.axis_index("v"), lax.axis_index("u")
    tiles = x_ref[...].reshape(2, 4, 4, 3, 8, LANES)
    made = exchange_lanes([tiles[:, :, i, :2].reshape(128, LANES) for i in range(4)])
    for tb in range(4):
        block = made[tb].reshape(2, 4, 2, 8, LANES)
        for q in range(4):
            a_ref[:, :, tb, :, q * LANES : (q + 1) * LANES] = block[:, q]
    made = exchange_lanes([tiles[0, :, i, 2].reshape(32, LANES) for i in range(4)])
    for b in range(2):
        block = made[b].reshape(4, 8, LANES)
        for q in range(4):
            r_ref[b, :, q * LANES : (q + 1) * LANES] = block[q]
    decays = r_ref[...].reshape(16, BLOCK)
    scaled = jnp.sqrt(1.0 - decays * decays)

    place = lax.axis_index(("l", "z"))
    marks = []
    for b in range(2):
        line = class_ref[pl.ds((u * 2 + b) * 4 + v * 2 + c, 1), :]
        marks.append(class_marks(line, place * 8, 8))
    mask = jnp.concatenate(marks * 8, axis=0) > 0.5
    matrices = (h0, l0, h1, l1)
    lines = a_ref[...].reshape(128, BLOCK)
    smoothed = lines + own_first(solve(lines, mask, matrices, False), v, c)
    smoothed = smoothed.reshape(2, 2, 2, 16, BLOCK)
    state, field = None, []
    for t in range(8):
        far, late, core = t // 4, (t // 2) % 2, t % 2
        pair = smoothed[far]
        pair = jnp.where(v == 0, pair[late], pair[1 - late])
        here = scaled * jnp.where(c == 0, pair[core], pair[1 - core])
        state = here if state is None else decays * state + here
        field.append(state)
    state, back = None, [None] * 8
    for t in range(7, -1, -1):
        here = scaled * field[t]
        state = here if state is None else decays * state + here
        back[t] = state
    back = jnp.concatenate(back, axis=0)
    adjoint = back + solve(own_first(back, v, c), mask, matrices, True)
    field = jnp.concatenate(field, axis=0).reshape(4, 4, 8, BLOCK)
    adjoint = adjoint.reshape(4, 4, 8, BLOCK)
    for core in range(2):
        for q in range(4):
            lanes = slice(q * LANES, (q + 1) * LANES)
            tiles = [
                value[:, core * 2 + b, :, lanes].reshape(32, LANES)
                for value in (field, adjoint)
                for b in range(2)
            ]
            made = exchange_lanes(tiles)
            for i in range(4):
                block = made[i].reshape(4, 8, LANES)
                for x in range(4):
                    out_ref[(q * 4 + i) * 8 + x * 2 + core] = block[x]


def last_kernel(x_ref, class_ref, h0, l0, h1, l1, field_ref, adjoint_ref):
    c, v = lax.axis_index("c"), lax.axis_index("v")
    tiles = x_ref[...].reshape(16, 8, 8, LANES)
    lines = []
    for u in range(2):
        pieces = []
        for k in range(4):
            turned = tiles[:, u * 4 + k].reshape(LANES, LANES).T
            for b in range(2):
                at = (u * 2 + b) * BLOCK + k * LANES
                field_ref[0, :, at : at + LANES] = turned[b * PIECE : (b + 1) * PIECE]
            pieces.append(turned[2 * PIECE :])
        lines.append(jnp.concatenate(pieces, axis=1))
    lines = jnp.concatenate(lines, axis=0)
    mask = row_mask(class_ref, 4)
    solved = lines + solve(own_first(lines, v, c), mask, (h0, l0, h1, l1), True)
    for b in range(4):
        piece = solved[b * PIECE : (b + 1) * PIECE]
        adjoint_ref[0, :, b * BLOCK : (b + 1) * BLOCK] = piece


def call(kernel, name, shapes, operands, smem=(), scratch=()):
    vmem = pl.BlockSpec(memory_space=pltpu.VMEM)
    places = [
        pl.BlockSpec(memory_space=pltpu.SMEM) if k in smem else vmem
        for k in range(len(operands))
    ]
    return pl.pallas_call(
        kernel,
        out_shape=tuple(jax.ShapeDtypeStruct(*shape) for shape in shapes),
        in_specs=places,
        out_specs=(vmem,) * len(shapes),
        scratch_shapes=[pltpu.VMEM(shape, F32) for shape in scratch],
        compiler_params=pltpu.CompilerParams(vmem_limit_bytes=40 * 1024 * 1024),
        name=name,
    )(*operands)


def swap(values, axis):
    return lax.all_to_all(values, axis, split_axis=0, concat_axis=0, tiled=True)


OTHER = [(0, 1), (1, 0)]


def partners(values):
    near = lax.ppermute(values, "v", OTHER)
    core = lax.ppermute(values, "c", OTHER)
    return core, near, lax.ppermute(near, "c", OTHER)


def from_sides(first, second):
    count = lax.axis_size("u") * 2
    up = [(k, (k + 1) % count) for k in range(count)]
    near = lax.ppermute(first, ("u", "v"), up)
    far = lax.ppermute(second, ("u", "v"), [(b, a) for a, b in up])
    return near, far


def per_device(forcing, rate_class, rate_table, row_class, col_class, offsets):
    row_lines = row_class.reshape(-1, LANES)
    col_lines = col_class.reshape(-1, LANES)

    quarter = lax.axis_index("v") * 2 + lax.axis_index("c")
    rows = offsets.shape[1]
    piece = lax.dynamic_slice(offsets, (0, 0, quarter * LANES), (2, rows, LANES))
    piece = piece.reshape(2 * rows, LANES)
    own = swap(jnp.broadcast_to(piece, (BLOCK // rows, 2 * rows, LANES)), ROWS)

    shapes = (((1024, BLOCK), BF16), ((512, LANES), F32), ((32, 8, LANES), F32))
    operands = (forcing,) + partners(forcing) + (rate_class, rate_table)
    lines = call(lines_kernel, "lines", shapes, operands, smem=(5,))
    own, *lines = lax.optimization_barrier((own,) + lines)
    own = own.reshape(-1, 2, rows, LANES)
    half = (own.shape[0] // 2,) + own.shape[1:]

    shapes = (((32, 3, 8, LANES), F32),) + (((BLOCK, 256), BF16),) * 2
    shapes += ((half, F32),) * 2
    operands = (*lines, own, row_lines)
    out, high, low, first, second = call(rows_kernel, "rows", shapes, operands)
    core = lax.ppermute(own, "c", OTHER)
    near = from_sides(first, second)
    both = [lax.ppermute(part, "c", OTHER) for part in near]
    own = (high, low)
    out = swap(out, NEAR)
    shapes = (((2, BLOCK, 384), BF16),) * 2
    rest = call(rest_kernel, "rest", shapes, (core, *near, *both))
    out, *rest = lax.optimization_barrier((out,) + rest)
    matrices = (*own, *rest)
    (out,) = call(
        middle_kernel,
        "middle",
        (((128, 8, LANES), F32),),
        (out, col_lines) + matrices,
        scratch=((2, 2, 4, 8, BLOCK), (2, 8, BLOCK)),
    )
    out = swap(out, SPREAD)
    shapes = ((forcing.shape, F32),) * 2
    return call(last_kernel, "last", shapes, (out, row_lines) + matrices)


def solution(mesh):
    devices = mesh.devices
    tm, row = devices.shape
    fine = Mesh(
        devices.reshape(tm // 4, 2, 2, row // 16, 2, 8), ("u", "v", "c", "h", "l", "z")
    )
    field = P(TIME, ROWS, None)
    return jax.shard_map(
        per_device,
        mesh=fine,
        in_specs=(field, P(ROWS, None), P(), P(), P(), P(None, ROWS, None)),
        out_specs=(field, field),
        check_vma=False,
    )
```

```python
import jax
import jax.numpy as jnp
from jax import lax
from jax.experimental import pallas as pl
from jax.experimental.pallas import tpu as pltpu
from jax.sharding import Mesh
from jax.sharding import PartitionSpec as P

BLOCK = 512
LANES = 128
PIECE = 32
F32 = jnp.float32
BF16 = jnp.bfloat16
ROWS = ("h", "l", "z")
TIME = ("x", "c")
NEAR = ("x", "l", "z")
SPREAD = ("x", "c", "l", "z")
SIDES = ((0, 3), (1, 2))


def place_along_x():
    x = lax.axis_index("x")
    u = x // 2
    return u, jnp.where(lax.rem(x, 2) == u, 0, 1)


def split(values):
    high = values.astype(BF16)
    return high, (values - high.astype(F32)).astype(BF16)


def product(both, high, low, adjoint):
    dims = (((1,), (1 if adjoint else 0,)), ((), ()))
    count = both.shape[0] // 2
    wide = lax.dot_general(both, high, dims, preferred_element_type=F32)
    small = lax.dot_general(both[:count], low, dims, preferred_element_type=F32)
    return wide[:count] + (wide[count:] + small)


def own_first(lines, v, c):
    quarters = [lines[:, k * LANES : (k + 1) * LANES] for k in range(4)]
    quarters = [jnp.where(v == 0, quarters[k], quarters[(k + 2) % 4]) for k in range(4)]
    quarters = [jnp.where(c == 0, quarters[k], quarters[k ^ 1]) for k in range(4)]
    return jnp.concatenate(quarters, axis=1)


def matrix(own_ref, rest_ref, k):
    return jnp.concatenate([own_ref[:, k * LANES : (k + 1) * LANES], rest_ref[k]], axis=1)


def solve(lines, mask, matrices, adjoint):
    own_high, own_low, rest_high, rest_low = matrices
    both = jnp.concatenate(split(lines), axis=0)
    parts = []
    for k in range(2):
        high, low = matrix(own_high, rest_high, k), matrix(own_low, rest_low, k)
        parts.append(product(both, high, low, adjoint))
    return jnp.where(mask, parts[0], parts[1])


def exchange_lanes(tiles):
    group = lax.broadcasted_iota(jnp.int32, tiles[0].shape, 1) // PIECE
    out = []
    for place in range(4):
        made = None
        for source in range(4):
            turn = ((source - place) % 4) * PIECE
            rolled = pltpu.roll(tiles[source], turn, 1) if turn else tiles[source]
            made = rolled if made is None else jnp.where(group == source, rolled, made)
        out.append(made)
    return out


def class_marks(line, first, count):
    lane = lax.broadcasted_iota(jnp.int32, (count, LANES), 1)
    row = lax.broadcasted_iota(jnp.int32, (count, LANES), 0)
    picked = jnp.where((lane == row + first) & (line == 0), 1.0, 0.0)
    return jnp.sum(picked, axis=1, keepdims=True)


def row_mask(class_ref, copies):
    place = lax.axis_index(ROWS)
    line = class_ref[pl.ds(place // 4, 1), :]
    marks = class_marks(line, lax.rem(place, 4) * PIECE, PIECE)
    return jnp.concatenate([marks] * copies, axis=0) > 0.5


def lines_kernel(f0, f1, f2, f3, rate_ref, table_ref, both_ref, same_ref, decays_ref):
    quarter = place_along_x()[1] * 2 + lax.axis_index("c")
    fields = ((f0, f1), (f2, f3))
    at = [pl.multiple_of(b * BLOCK + quarter * LANES, LANES) for b in range(4)]
    for far in range(2):
        for pair in range(2):
            for core in range(2):
                for b in range(2):
                    ref, block = fields[far][core], pair * 2 + b
                    first = (((far * 2 + pair) * 2 + core) * 2 + b) * PIECE
                    rows = pl.ds(first, PIECE)
                    lines = ref[0, :, block * BLOCK : (block + 1) * BLOCK]
                    high, low = split(lines)
                    both_ref[rows, :] = high
                    both_ref[pl.ds(512 + first, PIECE), :] = low
                    same_ref[rows, :] = ref[0, :, pl.ds(at[block], LANES)]
    for pair in range(2):
        rate = [rate_ref[:, pl.ds(at[pair * 2 + b], LANES)] for b in range(2)]
        rate = jnp.concatenate(rate, axis=0)
        decays = jnp.zeros(rate.shape, F32)
        for k in range(16):
            decays = jnp.where(rate == k, table_ref[k], decays)
        decays = jnp.concatenate([decays, decays], axis=0).T.reshape(16, 8, LANES)
        decays_ref[pair * 16 : (pair + 1) * 16] = decays


def rows_kernel(
    both_ref, same_ref, decays_ref, m_ref, class_ref, out_ref, high_ref, low_ref
):
    for k in range(2):
        high, low = split(m_ref[:, k].reshape(BLOCK, LANES))
        high_ref[:, k * LANES : (k + 1) * LANES] = high
        low_ref[:, k * LANES : (k + 1) * LANES] = low
    solved = product(both_ref[...], high_ref[...], low_ref[...], False)
    solved = jnp.where(row_mask(class_ref, 16), solved[:, :LANES], solved[:, LANES:])
    solved = solved + same_ref[...]
    for pair in range(2):
        at = slice(pair * 16, (pair + 1) * 16)
        for far in range(2):
            first = (far * 2 + pair) * LANES
            turned = solved[first : first + LANES].T
            out_ref[at, far] = turned.reshape(16, 8, LANES)
        out_ref[at, 2] = decays_ref[at]


def rest_kernel(m1, m2, m3, high_ref, low_ref):
    for n, ref in enumerate((m1, m2, m3)):
        for k in range(2):
            high, low = split(ref[:, k].reshape(BLOCK, LANES))
            high_ref[k, :, n * LANES : (n + 1) * LANES] = high
            low_ref[k, :, n * LANES : (n + 1) * LANES] = low


def middle_kernel(x_ref, class_ref, h0, l0, h1, l1, out_ref, a_ref, r_ref):
    c = lax.axis_index("c")
    u, v = place_along_x()
    tiles = x_ref[...].reshape(2, 4, 4, 3, 8, LANES)
    made = exchange_lanes([tiles[:, :, i, :2].reshape(128, LANES) for i in range(4)])
    for tb in range(4):
        block = made[tb].reshape(2, 4, 2, 8, LANES)
        for q in range(4):
            a_ref[:, :, tb, :, q * LANES : (q + 1) * LANES] = block[:, q]
    made = exchange_lanes([tiles[0, :, i, 2].reshape(32, LANES) for i in range(4)])
    for b in range(2):
        block = made[b].reshape(4, 8, LANES)
        for q in range(4):
            r_ref[b, :, q * LANES : (q + 1) * LANES] = block[q]
    decays = r_ref[...].reshape(16, BLOCK)
    scaled = jnp.sqrt(1.0 - decays * decays)

    place = lax.axis_index(("l", "z"))
    marks = []
    for b in range(2):
        line = class_ref[pl.ds((u * 2 + b) * 4 + v * 2 + c, 1), :]
        marks.append(class_marks(line, place * 8, 8))
    mask = jnp.concatenate(marks * 8, axis=0) > 0.5
    matrices = (h0, l0, h1, l1)
    lines = a_ref[...].reshape(128, BLOCK)
    smoothed = lines + own_first(solve(lines, mask, matrices, False), v, c)
    smoothed = smoothed.reshape(2, 2, 2, 16, BLOCK)
    state, field = None, []
    for t in range(8):
        far, late, core = t // 4, (t // 2) % 2, t % 2
        pair = smoothed[far]
        pair = jnp.where(v == far, pair[late], pair[1 - late])
        here = scaled * jnp.where(c == 0, pair[core], pair[1 - core])
        state = here if state is None else decays * state + here
        field.append(state)
    state, back = None, [None] * 8
    for t in range(7, -1, -1):
        here = scaled * field[t]
        state = here if state is None else decays * state + here
        back[t] = state
    back = jnp.concatenate(back, axis=0)
    adjoint = back + solve(own_first(back, v, c), mask, matrices, True)
    field = jnp.concatenate(field, axis=0).reshape(4, 4, 8, BLOCK)
    adjoint = adjoint.reshape(4, 4, 8, BLOCK)
    for core in range(2):
        for q in range(4):
            lanes = slice(q * LANES, (q + 1) * LANES)
            tiles = [
                value[:, core * 2 + b, :, lanes].reshape(32, LANES)
                for value in (field, adjoint)
                for b in range(2)
            ]
            made = exchange_lanes(tiles)
            for i in range(4):
                block = made[i].reshape(4, 8, LANES)
                for x in range(4):
                    out_ref[(x * 2 + core) * 16 + q * 4 + i] = block[x]


def last_kernel(
    x_ref, class_ref, h0, l0, h1, l1, field_out, adjoint_ref, field_ref, done
):
    c = lax.axis_index("c")
    v = place_along_x()[1]
    lines = []
    for u in range(2):
        pieces = []
        for k in range(4):
            first = ((u * 2 + ((k // 2) ^ u)) * 2 + k % 2) * 16
            turned = x_ref[first : first + 16].reshape(LANES, LANES).T
            for b in range(2):
                at = (u * 2 + b) * BLOCK + k * LANES
                field_ref[0, :, at : at + LANES] = turned[b * PIECE : (b + 1) * PIECE]
            pieces.append(turned[2 * PIECE :])
        lines.append(jnp.concatenate(pieces, axis=1))
    copy = pltpu.make_async_copy(field_ref, field_out, done)
    copy.start()
    lines = jnp.concatenate(lines, axis=0)
    mask = row_mask(class_ref, 4)
    solved = lines + solve(own_first(lines, v, c), mask, (h0, l0, h1, l1), True)
    for b in range(4):
        piece = solved[b * PIECE : (b + 1) * PIECE]
        adjoint_ref[0, :, b * BLOCK : (b + 1) * BLOCK] = piece
    copy.wait()


def call(kernel, name, shapes, operands, smem=(), scratch=(), loose=()):
    vmem = pl.BlockSpec(memory_space=pltpu.VMEM)
    places = [
        pl.BlockSpec(memory_space=pltpu.SMEM) if k in smem else vmem
        for k in range(len(operands))
    ]
    return pl.pallas_call(
        kernel,
        out_shape=tuple(jax.ShapeDtypeStruct(*shape) for shape in shapes),
        in_specs=places,
        out_specs=tuple(
            pl.BlockSpec(memory_space=pl.ANY) if k in loose else vmem
            for k in range(len(shapes))
        ),
        scratch_shapes=[pltpu.VMEM(shape, F32) for shape in scratch]
        + [pltpu.SemaphoreType.DMA] * len(loose),
        compiler_params=pltpu.CompilerParams(vmem_limit_bytes=40 * 1024 * 1024),
        name=name,
    )(*operands)


def swap(values, axis, groups=None):
    return lax.all_to_all(
        values, axis, split_axis=0, concat_axis=0, axis_index_groups=groups, tiled=True
    )


def partners(values):
    near = lax.ppermute(values, "x", [(k, k ^ 1) for k in range(4)])
    other = [(0, 1), (1, 0)]
    core = lax.ppermute(values, "c", other)
    return core, near, lax.ppermute(near, "c", other)


def per_device(forcing, rate_class, rate_table, row_class, col_class, offsets):
    row_lines = row_class.reshape(-1, LANES)
    col_lines = col_class.reshape(-1, LANES)

    quarter = place_along_x()[1] * 2 + lax.axis_index("c")
    rows = offsets.shape[1]
    piece = lax.dynamic_slice(offsets, (0, 0, quarter * LANES), (2, rows, LANES))
    piece = piece.reshape(2 * rows, LANES)
    own = swap(jnp.broadcast_to(piece, (BLOCK // rows, 2 * rows, LANES)), ROWS)

    shapes = (((1024, BLOCK), BF16), ((512, LANES), F32), ((32, 8, LANES), F32))
    operands = (forcing,) + partners(forcing) + (rate_class, rate_table)
    lines = call(lines_kernel, "lines", shapes, operands, smem=(5,))
    own, *lines = lax.optimization_barrier((own,) + lines)
    own = own.reshape(-1, 2, rows, LANES)
    rest = partners(own)

    shapes = (((32, 3, 8, LANES), F32),) + (((BLOCK, 256), BF16),) * 2
    operands = (*lines, own, row_lines)
    out, *own = call(rows_kernel, "rows", shapes, operands)
    count = lax.axis_size(("l", "z"))
    groups = [[x * count + k for x in side for k in range(count)] for side in SIDES]
    out = swap(out, NEAR, groups)
    shapes = (((2, BLOCK, 384), BF16),) * 2
    rest = call(rest_kernel, "rest", shapes, rest)
    out, *rest = lax.optimization_barrier((out,) + rest)
    matrices = (*own, *rest)
    (out,) = call(
        middle_kernel,
        "middle",
        (((128, 8, LANES), F32),),
        (out, col_lines) + matrices,
        scratch=((2, 2, 4, 8, BLOCK), (2, 8, BLOCK)),
    )
    out = swap(out, SPREAD)
    shapes = ((forcing.shape, F32),) * 2
    operands = (out, row_lines) + matrices
    scratch = (forcing.shape,)
    return call(last_kernel, "last", shapes, operands, scratch=scratch, loose=(0,))


def solution(mesh):
    devices = mesh.devices
    tm, row = devices.shape
    fine = Mesh(
        devices.reshape(tm // 2, 2, row // 16, 2, 8), ("x", "c", "h", "l", "z")
    )
    field = P(TIME, ROWS, None)
    return jax.shard_map(
        per_device,
        mesh=fine,
        in_specs=(field, P(ROWS, None), P(), P(), P(), P(None, ROWS, None)),
        out_specs=(field, field),
        check_vma=False,
    )
```

```python
import jax
import jax.numpy as jnp
from jax import lax
from jax.experimental import pallas as pl
from jax.experimental.pallas import tpu as pltpu
from jax.sharding import Mesh
from jax.sharding import PartitionSpec as P

BLOCK = 512
LANES = 128
PIECE = 32
F32 = jnp.float32
BF16 = jnp.bfloat16
ROWS = ("h", "l", "z")
TIME = ("x", "c")
NEAR = ("x", "l", "z")
SPREAD = ("x", "c", "l", "z")
SIDES = ((0, 3), (1, 2))


def place_along_x():
    x = lax.axis_index("x")
    u = x // 2
    return u, jnp.where(lax.rem(x, 2) == u, 0, 1)


def split(values):
    high = values.astype(BF16)
    return high, (values - high.astype(F32)).astype(BF16)


def product(both, high, low, adjoint):
    dims = (((1,), (1 if adjoint else 0,)), ((), ()))
    count = both.shape[0] // 2
    wide = lax.dot_general(both, high, dims, preferred_element_type=F32)
    small = lax.dot_general(both[:count], low, dims, preferred_element_type=F32)
    return wide[:count] + (wide[count:] + small)


def own_first(lines, v, c):
    quarters = [lines[:, k * LANES : (k + 1) * LANES] for k in range(4)]
    quarters = [jnp.where(v == 0, quarters[k], quarters[(k + 2) % 4]) for k in range(4)]
    quarters = [jnp.where(c == 0, quarters[k], quarters[k ^ 1]) for k in range(4)]
    return jnp.concatenate(quarters, axis=1)


def matrix(own_ref, rest_ref, k):
    return jnp.concatenate([own_ref[:, k * LANES : (k + 1) * LANES], rest_ref[k]], axis=1)


def solve(lines, mask, matrices, adjoint):
    own_high, own_low, rest_high, rest_low = matrices
    both = jnp.concatenate(split(lines), axis=0)
    parts = []
    for k in range(2):
        high, low = matrix(own_high, rest_high, k), matrix(own_low, rest_low, k)
        parts.append(product(both, high, low, adjoint))
    return jnp.where(mask, parts[0], parts[1])


def exchange_lanes(tiles):
    group = lax.broadcasted_iota(jnp.int32, tiles[0].shape, 1) // PIECE
    out = []
    for place in range(4):
        made = None
        for source in range(4):
            turn = ((source - place) % 4) * PIECE
            rolled = pltpu.roll(tiles[source], turn, 1) if turn else tiles[source]
            made = rolled if made is None else jnp.where(group == source, rolled, made)
        out.append(made)
    return out


def class_marks(line, first, count):
    lane = lax.broadcasted_iota(jnp.int32, (count, LANES), 1)
    row = lax.broadcasted_iota(jnp.int32, (count, LANES), 0)
    picked = jnp.where((lane == row + first) & (line == 0), 1.0, 0.0)
    return jnp.sum(picked, axis=1, keepdims=True)


def row_mask(class_ref, copies):
    place = lax.axis_index(ROWS)
    line = class_ref[pl.ds(place // 4, 1), :]
    marks = class_marks(line, lax.rem(place, 4) * PIECE, PIECE)
    return jnp.concatenate([marks] * copies, axis=0) > 0.5


def lines_kernel(f0, f1, f2, f3, rate_ref, table_ref, both_ref, same_ref, decays_ref):
    quarter = place_along_x()[1] * 2 + lax.axis_index("c")
    fields = ((f0, f1), (f2, f3))
    at = [pl.multiple_of(b * BLOCK + quarter * LANES, LANES) for b in range(4)]
    for far in range(2):
        for pair in range(2):
            for core in range(2):
                for b in range(2):
                    ref, block = fields[far][core], pair * 2 + b
                    first = (((far * 2 + pair) * 2 + core) * 2 + b) * PIECE
                    rows = pl.ds(first, PIECE)
                    lines = ref[0, :, block * BLOCK : (block + 1) * BLOCK]
                    high, low = split(lines)
                    both_ref[rows, :] = high
                    both_ref[pl.ds(512 + first, PIECE), :] = low
                    same_ref[rows, :] = ref[0, :, pl.ds(at[block], LANES)]
    for pair in range(2):
        rate = [rate_ref[:, pl.ds(at[pair * 2 + b], LANES)] for b in range(2)]
        rate = jnp.concatenate(rate, axis=0)
        decays = jnp.zeros(rate.shape, F32)
        for k in range(16):
            decays = jnp.where(rate == k, table_ref[k], decays)
        decays = jnp.concatenate([decays, decays], axis=0).T.reshape(16, 8, LANES)
        decays_ref[pair * 16 : (pair + 1) * 16] = decays


def rows_kernel(
    both_ref, same_ref, decays_ref, m_ref, class_ref, out_ref, high_ref, low_ref
):
    for k in range(2):
        high, low = split(m_ref[:, k].reshape(BLOCK, LANES))
        high_ref[:, k * LANES : (k + 1) * LANES] = high
        low_ref[:, k * LANES : (k + 1) * LANES] = low
    solved = product(both_ref[...], high_ref[...], low_ref[...], False)
    solved = jnp.where(row_mask(class_ref, 16), solved[:, :LANES], solved[:, LANES:])
    solved = solved + same_ref[...]
    for pair in range(2):
        at = slice(pair * 16, (pair + 1) * 16)
        for far in range(2):
            first = (far * 2 + pair) * LANES
            turned = solved[first : first + LANES].T
            out_ref[at, far] = turned.reshape(16, 8, LANES)
        out_ref[at, 2] = decays_ref[at]


def rest_kernel(m1, m2, m3, high_ref, low_ref):
    for n, ref in enumerate((m1, m2, m3)):
        for k in range(2):
            high, low = split(ref[:, k].reshape(BLOCK, LANES))
            high_ref[k, :, n * LANES : (n + 1) * LANES] = high
            low_ref[k, :, n * LANES : (n + 1) * LANES] = low


def middle_kernel(x_ref, class_ref, h0, l0, h1, l1, out_ref, a_ref, r_ref):
    c = lax.axis_index("c")
    u, v = place_along_x()
    tiles = x_ref[...].reshape(2, 4, 4, 3, 8, LANES)
    made = exchange_lanes([tiles[:, :, i, :2].reshape(128, LANES) for i in range(4)])
    for tb in range(4):
        block = made[tb].reshape(2, 4, 2, 8, LANES)
        for q in range(4):
            a_ref[:, :, tb, :, q * LANES : (q + 1) * LANES] = block[:, q]
    made = exchange_lanes([tiles[0, :, i, 2].reshape(32, LANES) for i in range(4)])
    for b in range(2):
        block = made[b].reshape(4, 8, LANES)
        for q in range(4):
            r_ref[b, :, q * LANES : (q + 1) * LANES] = block[q]
    decays = r_ref[...].reshape(16, BLOCK)
    scaled = jnp.sqrt(1.0 - decays * decays)

    place = lax.axis_index(("l", "z"))
    marks = []
    for b in range(2):
        line = class_ref[pl.ds((u * 2 + b) * 4 + v * 2 + c, 1), :]
        marks.append(class_marks(line, place * 8, 8))
    mask = jnp.concatenate(marks * 8, axis=0) > 0.5
    matrices = (h0, l0, h1, l1)
    lines = a_ref[...].reshape(128, BLOCK)
    smoothed = lines + own_first(solve(lines, mask, matrices, False), v, c)
    smoothed = smoothed.reshape(2, 2, 2, 16, BLOCK)
    state, field = None, []
    for t in range(8):
        far, late, core = t // 4, (t // 2) % 2, t % 2
        pair = smoothed[far]
        pair = jnp.where(v == far, pair[late], pair[1 - late])
        here = scaled * jnp.where(c == 0, pair[core], pair[1 - core])
        state = here if state is None else decays * state + here
        field.append(state)
    state, back = None, [None] * 8
    for t in range(7, -1, -1):
        here = scaled * field[t]
        state = here if state is None else decays * state + here
        back[t] = state
    back = jnp.concatenate(back, axis=0)
    adjoint = back + solve(own_first(back, v, c), mask, matrices, True)
    field = jnp.concatenate(field, axis=0).reshape(4, 4, 8, BLOCK)
    adjoint = adjoint.reshape(4, 4, 8, BLOCK)
    for core in range(2):
        for q in range(4):
            lanes = slice(q * LANES, (q + 1) * LANES)
            tiles = [
                value[:, core * 2 + b, :, lanes].reshape(32, LANES)
                for value in (field, adjoint)
                for b in range(2)
            ]
            made = exchange_lanes(tiles)
            for i in range(4):
                block = made[i].reshape(4, 8, LANES)
                for x in range(4):
                    out_ref[(x * 2 + core) * 16 + q * 4 + i] = block[x]


def last_kernel(x_ref, class_ref, h0, l0, h1, l1, field_ref, adjoint_ref):
    c = lax.axis_index("c")
    v = place_along_x()[1]
    lines = []
    for u in range(2):
        pieces = []
        for k in range(4):
            first = ((u * 2 + ((k // 2) ^ u)) * 2 + k % 2) * 16
            turned = x_ref[first : first + 16].reshape(LANES, LANES).T
            for b in range(2):
                at = (u * 2 + b) * BLOCK + k * LANES
                field_ref[0, :, at : at + LANES] = turned[b * PIECE : (b + 1) * PIECE]
            pieces.append(turned[2 * PIECE :])
        lines.append(jnp.concatenate(pieces, axis=1))
    lines = jnp.concatenate(lines, axis=0)
    mask = row_mask(class_ref, 4)
    solved = lines + solve(own_first(lines, v, c), mask, (h0, l0, h1, l1), True)
    for b in range(4):
        piece = solved[b * PIECE : (b + 1) * PIECE]
        adjoint_ref[0, :, b * BLOCK : (b + 1) * BLOCK] = piece


def call(kernel, name, shapes, operands, smem=(), scratch=()):
    vmem = pl.BlockSpec(memory_space=pltpu.VMEM)
    places = [
        pl.BlockSpec(memory_space=pltpu.SMEM) if k in smem else vmem
        for k in range(len(operands))
    ]
    return pl.pallas_call(
        kernel,
        out_shape=tuple(jax.ShapeDtypeStruct(*shape) for shape in shapes),
        in_specs=places,
        out_specs=(vmem,) * len(shapes),
        scratch_shapes=[pltpu.VMEM(shape, F32) for shape in scratch],
        compiler_params=pltpu.CompilerParams(vmem_limit_bytes=40 * 1024 * 1024),
        name=name,
    )(*operands)


def swap(values, axis, groups=None):
    return lax.all_to_all(
        values, axis, split_axis=0, concat_axis=0, axis_index_groups=groups, tiled=True
    )


def partners(values):
    near = lax.ppermute(values, "x", [(k, k ^ 1) for k in range(4)])
    other = [(0, 1), (1, 0)]
    core = lax.ppermute(values, "c", other)
    return core, near, lax.ppermute(near, "c", other)


def per_device(forcing, rate_class, rate_table, row_class, col_class, offsets):
    row_lines = row_class.reshape(-1, LANES)
    col_lines = col_class.reshape(-1, LANES)

    quarter = place_along_x()[1] * 2 + lax.axis_index("c")
    rows = offsets.shape[1]
    piece = lax.dynamic_slice(offsets, (0, 0, quarter * LANES), (2, rows, LANES))
    piece = piece.reshape(2 * rows, LANES)
    own = swap(jnp.broadcast_to(piece, (BLOCK // rows, 2 * rows, LANES)), ROWS)

    shapes = (((1024, BLOCK), BF16), ((512, LANES), F32), ((32, 8, LANES), F32))
    operands = (forcing,) + partners(forcing) + (rate_class, rate_table)
    lines = call(lines_kernel, "lines", shapes, operands, smem=(5,))
    own, *lines = lax.optimization_barrier((own,) + lines)
    own = own.reshape(-1, 2, rows, LANES)
    rest = partners(own)

    shapes = (((32, 3, 8, LANES), F32),) + (((BLOCK, 256), BF16),) * 2
    operands = (*lines, own, row_lines)
    out, *own = call(rows_kernel, "rows", shapes, operands)
    count = lax.axis_size(("l", "z"))
    groups = [[x * count + k for x in side for k in range(count)] for side in SIDES]
    out = swap(out, NEAR, groups)
    shapes = (((2, BLOCK, 384), BF16),) * 2
    rest = call(rest_kernel, "rest", shapes, rest)
    out, *rest = lax.optimization_barrier((out,) + rest)
    matrices = (*own, *rest)
    (out,) = call(
        middle_kernel,
        "middle",
        (((128, 8, LANES), F32),),
        (out, col_lines) + matrices,
        scratch=((2, 2, 4, 8, BLOCK), (2, 8, BLOCK)),
    )
    out = swap(out, SPREAD)
    shapes = ((forcing.shape, F32),) * 2
    return call(last_kernel, "last", shapes, (out, row_lines) + matrices)


def solution(mesh):
    devices = mesh.devices
    tm, row = devices.shape
    fine = Mesh(
        devices.reshape(tm // 2, 2, row // 16, 2, 8), ("x", "c", "h", "l", "z")
    )
    field = P(TIME, ROWS, None)
    return jax.shard_map(
        per_device,
        mesh=fine,
        in_specs=(field, P(ROWS, None), P(), P(), P(), P(None, ROWS, None)),
        out_specs=(field, field),
        check_vma=False,
    )
```

```python
import jax
import jax.numpy as jnp
from jax import lax
from jax.experimental import pallas as pl
from jax.experimental.pallas import tpu as pltpu
from jax.sharding import Mesh
from jax.sharding import PartitionSpec as P

BLOCK = 512
LANES = 128
PIECE = 32
F32 = jnp.float32
BF16 = jnp.bfloat16
ROWS = ("h", "l", "z")
TIME = ("x", "c")
NEAR = ("x", "l", "z")
SPREAD = ("x", "c", "l", "z")
SIDES = ((0, 3), (1, 2))


def place_along_x():
    x, odd = lax.axis_index("x"), lax.rem(lax.axis_index("h"), 2)
    u = x // 2
    side = jnp.where(lax.rem(x, 2) == u, 0, 1)
    return u, jnp.where(side == odd, 0, 1), side, odd


def split(values):
    high = values.astype(BF16)
    return high, (values - high.astype(F32)).astype(BF16)


def product(both, high, low, adjoint):
    dims = (((1,), (1 if adjoint else 0,)), ((), ()))
    count = both.shape[0] // 2
    wide = lax.dot_general(both, high, dims, preferred_element_type=F32)
    small = lax.dot_general(both[:count], low, dims, preferred_element_type=F32)
    return wide[:count] + (wide[count:] + small)


def own_first(lines, v, c):
    quarters = [lines[:, k * LANES : (k + 1) * LANES] for k in range(4)]
    quarters = [jnp.where(v == 0, quarters[k], quarters[(k + 2) % 4]) for k in range(4)]
    quarters = [jnp.where(c == 0, quarters[k], quarters[k ^ 1]) for k in range(4)]
    return jnp.concatenate(quarters, axis=1)


def matrix(own_ref, rest_ref, k):
    return jnp.concatenate([own_ref[:, k * LANES : (k + 1) * LANES], rest_ref[k]], axis=1)


def solve(lines, mask, matrices, adjoint):
    own_high, own_low, rest_high, rest_low = matrices
    both = jnp.concatenate(split(lines), axis=0)
    parts = []
    for k in range(2):
        high, low = matrix(own_high, rest_high, k), matrix(own_low, rest_low, k)
        parts.append(product(both, high, low, adjoint))
    return jnp.where(mask, parts[0], parts[1])


def exchange_lanes(tiles):
    group = lax.broadcasted_iota(jnp.int32, tiles[0].shape, 1) // PIECE
    out = []
    for place in range(4):
        made = None
        for source in range(4):
            turn = ((source - place) % 4) * PIECE
            rolled = pltpu.roll(tiles[source], turn, 1) if turn else tiles[source]
            made = rolled if made is None else jnp.where(group == source, rolled, made)
        out.append(made)
    return out


def class_marks(line, first, count):
    lane = lax.broadcasted_iota(jnp.int32, (count, LANES), 1)
    row = lax.broadcasted_iota(jnp.int32, (count, LANES), 0)
    picked = jnp.where((lane == row + first) & (line == 0), 1.0, 0.0)
    return jnp.sum(picked, axis=1, keepdims=True)


def row_mask(class_ref, copies):
    place = lax.axis_index(ROWS)
    line = class_ref[pl.ds(place // 4, 1), :]
    marks = class_marks(line, lax.rem(place, 4) * PIECE, PIECE)
    return jnp.concatenate([marks] * copies, axis=0) > 0.5


def pieces_kernel(m_ref, out_ref):
    c, side = lax.axis_index("c"), place_along_x()[2]
    count = lax.axis_size(("l", "z"))
    pieces = []
    for v in (side, 1 - side):
        at = pl.multiple_of((v * 2 + c) * LANES, LANES)
        pieces.append(m_ref[:, :, pl.ds(at, LANES)].reshape(out_ref.shape[1:]))
    for device in range(out_ref.shape[0]):
        out_ref[device] = pieces[(device // count) % 2]


def lines_kernel(f0, f1, f2, f3, rate_ref, table_ref, both_ref, same_ref, decays_ref):
    quarter = place_along_x()[1] * 2 + lax.axis_index("c")
    fields = ((f0, f1), (f2, f3))
    at = [pl.multiple_of(b * BLOCK + quarter * LANES, LANES) for b in range(4)]
    for far in range(2):
        for pair in range(2):
            for core in range(2):
                for b in range(2):
                    ref, block = fields[far][core], pair * 2 + b
                    first = (((far * 2 + pair) * 2 + core) * 2 + b) * PIECE
                    rows = pl.ds(first, PIECE)
                    lines = ref[0, :, block * BLOCK : (block + 1) * BLOCK]
                    high, low = split(lines)
                    both_ref[rows, :] = high
                    both_ref[pl.ds(512 + first, PIECE), :] = low
                    same_ref[rows, :] = ref[0, :, pl.ds(at[block], LANES)]
    for pair in range(2):
        rate = [rate_ref[:, pl.ds(at[pair * 2 + b], LANES)] for b in range(2)]
        rate = jnp.concatenate(rate, axis=0)
        decays = jnp.zeros(rate.shape, F32)
        for k in range(16):
            decays = jnp.where(rate == k, table_ref[k], decays)
        decays = jnp.concatenate([decays, decays], axis=0).T.reshape(16, 8, LANES)
        decays_ref[pair * 16 : (pair + 1) * 16] = decays


def rows_kernel(
    both_ref, same_ref, decays_ref, m_ref, class_ref,
    out_ref, high_ref, low_ref, first_ref, second_ref,
):
    half = m_ref.shape[0] // 2
    first_ref[...] = m_ref[:half]
    second_ref[...] = m_ref[half:]
    for k in range(2):
        high, low = split(m_ref[:, k].reshape(BLOCK, LANES))
        high_ref[:, k * LANES : (k + 1) * LANES] = high
        low_ref[:, k * LANES : (k + 1) * LANES] = low
    solved = product(both_ref[...], high_ref[...], low_ref[...], False)
    solved = jnp.where(row_mask(class_ref, 16), solved[:, :LANES], solved[:, LANES:])
    solved = solved + same_ref[...]
    for pair in range(2):
        at = slice(pair * 16, (pair + 1) * 16)
        for far in range(2):
            first = (far * 2 + pair) * LANES
            turned = solved[first : first + LANES].T
            out_ref[at, far] = turned.reshape(16, 8, LANES)
        out_ref[at, 2] = decays_ref[at]


def rest_kernel(m1, near1, near2, both1, both2, high_ref, low_ref):
    for n, refs in enumerate(((m1,), (near1, near2), (both1, both2))):
        lanes = slice(n * LANES, (n + 1) * LANES)
        count = BLOCK // len(refs)
        for k in range(2):
            for part, ref in enumerate(refs):
                rows = slice(part * count, (part + 1) * count)
                high, low = split(ref[:, k].reshape(count, LANES))
                high_ref[k, rows, lanes] = high
                low_ref[k, rows, lanes] = low


def middle_kernel(x_ref, class_ref, h0, l0, h1, l1, out_ref, a_ref, r_ref):
    c = lax.axis_index("c")
    u, v, side, _ = place_along_x()
    tiles = x_ref[...].reshape(2, 4, 4, 3, 8, LANES)
    made = exchange_lanes([tiles[:, :, i, :2].reshape(128, LANES) for i in range(4)])
    for tb in range(4):
        block = made[tb].reshape(2, 4, 2, 8, LANES)
        for q in range(4):
            a_ref[:, :, tb, :, q * LANES : (q + 1) * LANES] = block[:, q]
    made = exchange_lanes([tiles[0, :, i, 2].reshape(32, LANES) for i in range(4)])
    for b in range(2):
        block = made[b].reshape(4, 8, LANES)
        for q in range(4):
            r_ref[b, :, q * LANES : (q + 1) * LANES] = block[q]
    decays = r_ref[...].reshape(16, BLOCK)
    scaled = jnp.sqrt(1.0 - decays * decays)

    place = lax.axis_index(("l", "z"))
    marks = []
    for b in range(2):
        line = class_ref[pl.ds((u * 2 + b) * 4 + v * 2 + c, 1), :]
        marks.append(class_marks(line, place * 8, 8))
    mask = jnp.concatenate(marks * 8, axis=0) > 0.5
    matrices = (h0, l0, h1, l1)
    lines = a_ref[...].reshape(128, BLOCK)
    smoothed = lines + own_first(solve(lines, mask, matrices, False), v, c)
    smoothed = smoothed.reshape(2, 2, 2, 16, BLOCK)
    state, field = None, []
    for t in range(8):
        far, late, core = t // 4, (t // 2) % 2, t % 2
        pair = smoothed[far]
        pair = jnp.where(side == far, pair[late], pair[1 - late])
        here = scaled * jnp.where(c == 0, pair[core], pair[1 - core])
        state = here if state is None else decays * state + here
        field.append(state)
    state, back = None, [None] * 8
    for t in range(7, -1, -1):
        here = scaled * field[t]
        state = here if state is None else decays * state + here
        back[t] = state
    back = jnp.concatenate(back, axis=0)
    adjoint = back + solve(own_first(back, v, c), mask, matrices, True)
    field = jnp.concatenate(field, axis=0).reshape(4, 4, 8, BLOCK)
    adjoint = adjoint.reshape(4, 4, 8, BLOCK)
    for core in range(2):
        for q in range(4):
            lanes = slice(q * LANES, (q + 1) * LANES)
            tiles = [
                value[:, core * 2 + b, :, lanes].reshape(32, LANES)
                for value in (field, adjoint)
                for b in range(2)
            ]
            made = exchange_lanes(tiles)
            for i in range(4):
                block = made[i].reshape(4, 8, LANES)
                for x in range(4):
                    out_ref[(x * 2 + core) * 16 + q * 4 + i] = block[x]


def last_kernel(x_ref, class_ref, h0, l0, h1, l1, field_ref, adjoint_ref):
    c = lax.axis_index("c")
    _, v, _, odd = place_along_x()
    lines = []
    for u in range(2):
        pieces = []
        for k in range(4):
            turn = (k // 2) ^ u
            x = u * 2 + jnp.where(odd == 0, turn, 1 - turn)
            first = pl.multiple_of((x * 2 + k % 2) * 16, 16)
            turned = x_ref[pl.ds(first, 16)].reshape(LANES, LANES).T
            for b in range(2):
                at = (u * 2 + b) * BLOCK + k * LANES
                field_ref[0, :, at : at + LANES] = turned[b * PIECE : (b + 1) * PIECE]
            pieces.append(turned[2 * PIECE :])
        lines.append(jnp.concatenate(pieces, axis=1))
    lines = jnp.concatenate(lines, axis=0)
    mask = row_mask(class_ref, 4)
    solved = lines + solve(own_first(lines, v, c), mask, (h0, l0, h1, l1), True)
    for b in range(4):
        piece = solved[b * PIECE : (b + 1) * PIECE]
        adjoint_ref[0, :, b * BLOCK : (b + 1) * BLOCK] = piece


def call(kernel, name, shapes, operands, smem=(), scratch=()):
    vmem = pl.BlockSpec(memory_space=pltpu.VMEM)
    places = [
        pl.BlockSpec(memory_space=pltpu.SMEM) if k in smem else vmem
        for k in range(len(operands))
    ]
    return pl.pallas_call(
        kernel,
        out_shape=tuple(jax.ShapeDtypeStruct(*shape) for shape in shapes),
        in_specs=places,
        out_specs=(vmem,) * len(shapes),
        scratch_shapes=[pltpu.VMEM(shape, F32) for shape in scratch],
        compiler_params=pltpu.CompilerParams(vmem_limit_bytes=40 * 1024 * 1024),
        name=name,
    )(*operands)


def swap(values, axis, groups=None):
    return lax.all_to_all(
        values, axis, split_axis=0, concat_axis=0, axis_index_groups=groups, tiled=True
    )


def from_core(values):
    return lax.ppermute(values, "c", [(0, 1), (1, 0)])


def from_near(values):
    return lax.ppermute(values, "x", [(k, k ^ 1) for k in range(4)])


def from_next(values):
    count = lax.axis_size("h") * 2
    pairs = [(k, (k + 1) % count) for k in range(1, count, 2)]
    return lax.ppermute(values, ("h", "l"), pairs + [(b, a) for a, b in pairs])


def per_device(forcing, rate_class, rate_table, row_class, col_class, offsets):
    row_lines = row_class.reshape(-1, LANES)
    col_lines = col_class.reshape(-1, LANES)

    rows = offsets.shape[1]
    shape = (BLOCK // rows, 2 * rows, LANES)
    (own,) = call(pieces_kernel, "pieces", ((shape, F32),), (offsets,))
    own = swap(own, ROWS)

    shapes = (((1024, BLOCK), BF16), ((512, LANES), F32), ((32, 8, LANES), F32))
    near = from_near(forcing)
    fields = (forcing, from_core(forcing), near, from_core(near))
    operands = fields + (rate_class, rate_table)
    lines = call(lines_kernel, "lines", shapes, operands, smem=(5,))
    own, *lines = lax.optimization_barrier((own,) + lines)
    own = own.reshape(-1, 2, rows, LANES)
    half = (own.shape[0] // 2,) + own.shape[1:]

    shapes = (((32, 3, 8, LANES), F32),) + (((BLOCK, 256), BF16),) * 2
    shapes += ((half, F32),) * 2
    operands = (*lines, own, row_lines)
    out, high, low, first, second = call(rows_kernel, "rows", shapes, operands)
    near = (from_near(first), from_next(second))
    rest = (from_core(own), *near, *map(from_core, near))
    own = (high, low)
    count = lax.axis_size(("l", "z"))
    groups = [[x * count + k for x in side for k in range(count)] for side in SIDES]
    out = swap(out, NEAR, groups)
    shapes = (((2, BLOCK, 384), BF16),) * 2
    rest = call(rest_kernel, "rest", shapes, rest)
    out, *rest = lax.optimization_barrier((out,) + rest)
    matrices = (*own, *rest)
    (out,) = call(
        middle_kernel,
        "middle",
        (((128, 8, LANES), F32),),
        (out, col_lines) + matrices,
        scratch=((2, 2, 4, 8, BLOCK), (2, 8, BLOCK)),
    )
    out = swap(out, SPREAD)
    shapes = ((forcing.shape, F32),) * 2
    return call(last_kernel, "last", shapes, (out, row_lines) + matrices)


def solution(mesh):
    devices = mesh.devices
    tm, row = devices.shape
    fine = Mesh(
        devices.reshape(tm // 2, 2, row // 16, 2, 8), ("x", "c", "h", "l", "z")
    )
    field = P(TIME, ROWS, None)
    return jax.shard_map(
        per_device,
        mesh=fine,
        in_specs=(field, P(ROWS, None), P(), P(), P(), P(None, ROWS, None)),
        out_specs=(field, field),
        check_vma=False,
    )
```

```python
import jax
import jax.numpy as jnp
from jax import lax
from jax.experimental import pallas as pl
from jax.experimental.pallas import tpu as pltpu
from jax.sharding import Mesh
from jax.sharding import PartitionSpec as P

BLOCK = 512
LANES = 128
PIECE = 32
F32 = jnp.float32
BF16 = jnp.bfloat16
ROWS = ("h", "l", "z")
TIME = ("x", "c")
NEAR = ("x", "l", "z")
SPREAD = ("l", "z", "x", "c")
SHARDS = ("l", "h", "z")
SIDES = ((0, 3), (1, 2))


def place_along_x():
    x = lax.axis_index("x")
    u = x // 2
    return u, jnp.where(lax.rem(x, 2) == u, 0, 1)


def split(values):
    high = values.astype(BF16)
    return high, (values - high.astype(F32)).astype(BF16)


def product(both, high, low, adjoint):
    dims = (((1,), (1 if adjoint else 0,)), ((), ()))
    count = both.shape[0] // 2
    wide = lax.dot_general(both, high, dims, preferred_element_type=F32)
    small = lax.dot_general(both[:count], low, dims, preferred_element_type=F32)
    return wide[:count] + (wide[count:] + small)


def own_first(lines, v, c):
    quarters = [lines[:, k * LANES : (k + 1) * LANES] for k in range(4)]
    quarters = [jnp.where(v == 0, quarters[k], quarters[(k + 2) % 4]) for k in range(4)]
    quarters = [jnp.where(c == 0, quarters[k], quarters[k ^ 1]) for k in range(4)]
    return jnp.concatenate(quarters, axis=1)


def matrix(own_ref, rest_ref, k):
    return jnp.concatenate([own_ref[:, k * LANES : (k + 1) * LANES], rest_ref[k]], axis=1)


def solve(lines, mask, matrices, adjoint):
    own_high, own_low, rest_high, rest_low = matrices
    both = jnp.concatenate(split(lines), axis=0)
    parts = []
    for k in range(2):
        high, low = matrix(own_high, rest_high, k), matrix(own_low, rest_low, k)
        parts.append(product(both, high, low, adjoint))
    return jnp.where(mask, parts[0], parts[1])


def exchange_lanes(tiles):
    group = lax.broadcasted_iota(jnp.int32, tiles[0].shape, 1) // PIECE
    out = []
    for place in range(4):
        made = None
        for source in range(4):
            turn = ((source - place) % 4) * PIECE
            rolled = pltpu.roll(tiles[source], turn, 1) if turn else tiles[source]
            made = rolled if made is None else jnp.where(group == source, rolled, made)
        out.append(made)
    return out


def class_marks(line, first, count):
    lane = lax.broadcasted_iota(jnp.int32, (count, LANES), 1)
    row = lax.broadcasted_iota(jnp.int32, (count, LANES), 0)
    picked = jnp.where((lane == row + first) & (line == 0), 1.0, 0.0)
    return jnp.sum(picked, axis=1, keepdims=True)


def row_mask(class_ref, copies):
    place = lax.axis_index(ROWS)
    line = class_ref[pl.ds(place // 4, 1), :]
    marks = class_marks(line, lax.rem(place, 4) * PIECE, PIECE)
    return jnp.concatenate([marks] * copies, axis=0) > 0.5


def lines_kernel(f0, f1, f2, f3, rate_ref, table_ref, both_ref, same_ref, decays_ref):
    quarter = place_along_x()[1] * 2 + lax.axis_index("c")
    fields = ((f0, f1), (f2, f3))
    at = [pl.multiple_of(b * BLOCK + quarter * LANES, LANES) for b in range(4)]
    for far in range(2):
        for pair in range(2):
            for core in range(2):
                for b in range(2):
                    ref, block = fields[far][core], pair * 2 + b
                    first = (((far * 2 + pair) * 2 + core) * 2 + b) * PIECE
                    rows = pl.ds(first, PIECE)
                    lines = ref[0, :, block * BLOCK : (block + 1) * BLOCK]
                    high, low = split(lines)
                    both_ref[rows, :] = high
                    both_ref[pl.ds(512 + first, PIECE), :] = low
                    same_ref[rows, :] = ref[0, :, pl.ds(at[block], LANES)]
    for pair in range(2):
        rate = [rate_ref[:, pl.ds(at[pair * 2 + b], LANES)] for b in range(2)]
        rate = jnp.concatenate(rate, axis=0)
        decays = jnp.zeros(rate.shape, F32)
        for k in range(16):
            decays = jnp.where(rate == k, table_ref[k], decays)
        decays = jnp.concatenate([decays, decays], axis=0).T.reshape(16, 8, LANES)
        decays_ref[pair * 16 : (pair + 1) * 16] = decays


def rows_kernel(
    both_ref, same_ref, decays_ref, m_ref, class_ref, out_ref, high_ref, low_ref
):
    for k in range(2):
        high, low = split(in_rows(m_ref, k))
        high_ref[:, k * LANES : (k + 1) * LANES] = high
        low_ref[:, k * LANES : (k + 1) * LANES] = low
    solved = product(both_ref[...], high_ref[...], low_ref[...], False)
    solved = jnp.where(row_mask(class_ref, 16), solved[:, :LANES], solved[:, LANES:])
    solved = solved + same_ref[...]
    for pair in range(2):
        at = slice(pair * 16, (pair + 1) * 16)
        for far in range(2):
            first = (far * 2 + pair) * LANES
            turned = solved[first : first + LANES].T
            out_ref[at, far] = turned.reshape(16, 8, LANES)
        out_ref[at, 2] = decays_ref[at]


def in_rows(ref, k):
    outer, inner, run = (lax.axis_size(name) for name in SHARDS)
    starts = [(a * inner + b) * run for b in range(inner) for a in range(outer)]
    pieces = [ref[at : at + run, k].reshape(-1, LANES) for at in starts]
    return jnp.concatenate(pieces, axis=0)


def rest_kernel(m1, m2, m3, high_ref, low_ref):
    for n, ref in enumerate((m1, m2, m3)):
        for k in range(2):
            high, low = split(in_rows(ref, k))
            high_ref[k, :, n * LANES : (n + 1) * LANES] = high
            low_ref[k, :, n * LANES : (n + 1) * LANES] = low


def middle_kernel(x_ref, class_ref, h0, l0, h1, l1, out_ref, a_ref, r_ref):
    c = lax.axis_index("c")
    u, v = place_along_x()
    tiles = x_ref[...].reshape(2, 4, 4, 3, 8, LANES)
    made = exchange_lanes([tiles[:, :, i, :2].reshape(128, LANES) for i in range(4)])
    for tb in range(4):
        block = made[tb].reshape(2, 4, 2, 8, LANES)
        for q in range(4):
            a_ref[:, :, tb, :, q * LANES : (q + 1) * LANES] = block[:, q]
    made = exchange_lanes([tiles[0, :, i, 2].reshape(32, LANES) for i in range(4)])
    for b in range(2):
        block = made[b].reshape(4, 8, LANES)
        for q in range(4):
            r_ref[b, :, q * LANES : (q + 1) * LANES] = block[q]
    decays = r_ref[...].reshape(16, BLOCK)
    scaled = jnp.sqrt(1.0 - decays * decays)

    place = lax.axis_index(("l", "z"))
    marks = []
    for b in range(2):
        line = class_ref[pl.ds((u * 2 + b) * 4 + v * 2 + c, 1), :]
        marks.append(class_marks(line, place * 8, 8))
    mask = jnp.concatenate(marks * 8, axis=0) > 0.5
    matrices = (h0, l0, h1, l1)
    lines = a_ref[...].reshape(128, BLOCK)
    smoothed = lines + own_first(solve(lines, mask, matrices, False), v, c)
    smoothed = smoothed.reshape(2, 2, 2, 16, BLOCK)
    state, field = None, []
    for t in range(8):
        far, late, core = t // 4, (t // 2) % 2, t % 2
        pair = smoothed[far]
        pair = jnp.where(v == far, pair[late], pair[1 - late])
        here = scaled * jnp.where(c == 0, pair[core], pair[1 - core])
        state = here if state is None else decays * state + here
        field.append(state)
    state, back = None, [None] * 8
    for t in range(7, -1, -1):
        here = scaled * field[t]
        state = here if state is None else decays * state + here
        back[t] = state
    back = jnp.concatenate(back, axis=0)
    adjoint = back + solve(own_first(back, v, c), mask, matrices, True)
    field = jnp.concatenate(field, axis=0).reshape(4, 4, 8, BLOCK)
    adjoint = adjoint.reshape(4, 4, 8, BLOCK)
    for core in range(2):
        for q in range(4):
            lanes = slice(q * LANES, (q + 1) * LANES)
            tiles = [
                value[:, core * 2 + b, :, lanes].reshape(32, LANES)
                for value in (field, adjoint)
                for b in range(2)
            ]
            made = exchange_lanes(tiles)
            for i in range(4):
                block = made[i].reshape(4, 8, LANES)
                for x in range(4):
                    out_ref[(q * 4 + i) * 8 + x * 2 + core] = block[x]


def last_kernel(x_ref, class_ref, h0, l0, h1, l1, field_ref, adjoint_ref):
    c = lax.axis_index("c")
    v = place_along_x()[1]
    tiles = x_ref[...].reshape(16, 8, 8, LANES)
    lines = []
    for u in range(2):
        pieces = []
        for k in range(4):
            source = (u * 2 + ((k // 2) ^ u)) * 2 + k % 2
            turned = tiles[:, source].reshape(LANES, LANES).T
            for b in range(2):
                at = (u * 2 + b) * BLOCK + k * LANES
                field_ref[0, :, at : at + LANES] = turned[b * PIECE : (b + 1) * PIECE]
            pieces.append(turned[2 * PIECE :])
        lines.append(jnp.concatenate(pieces, axis=1))
    lines = jnp.concatenate(lines, axis=0)
    mask = row_mask(class_ref, 4)
    solved = lines + solve(own_first(lines, v, c), mask, (h0, l0, h1, l1), True)
    for b in range(4):
        piece = solved[b * PIECE : (b + 1) * PIECE]
        adjoint_ref[0, :, b * BLOCK : (b + 1) * BLOCK] = piece


def call(kernel, name, shapes, operands, smem=(), scratch=()):
    vmem = pl.BlockSpec(memory_space=pltpu.VMEM)
    places = [
        pl.BlockSpec(memory_space=pltpu.SMEM) if k in smem else vmem
        for k in range(len(operands))
    ]
    return pl.pallas_call(
        kernel,
        out_shape=tuple(jax.ShapeDtypeStruct(*shape) for shape in shapes),
        in_specs=places,
        out_specs=(vmem,) * len(shapes),
        scratch_shapes=[pltpu.VMEM(shape, F32) for shape in scratch],
        compiler_params=pltpu.CompilerParams(vmem_limit_bytes=40 * 1024 * 1024),
        name=name,
    )(*operands)


def swap(values, axis, groups=None):
    return lax.all_to_all(
        values, axis, split_axis=0, concat_axis=0, axis_index_groups=groups, tiled=True
    )


def partners(values):
    near = lax.ppermute(values, "x", [(k, k ^ 1) for k in range(4)])
    other = [(0, 1), (1, 0)]
    core = lax.ppermute(values, "c", other)
    return core, near, lax.ppermute(near, "c", other)


def per_device(forcing, rate_class, rate_table, row_class, col_class, offsets):
    row_lines = row_class.reshape(-1, LANES)
    col_lines = col_class.reshape(-1, LANES)

    quarter = place_along_x()[1] * 2 + lax.axis_index("c")
    rows = offsets.shape[1]
    piece = lax.dynamic_slice(offsets, (0, 0, quarter * LANES), (2, rows, LANES))
    piece = piece.reshape(2 * rows, LANES)
    own = swap(jnp.broadcast_to(piece, (BLOCK // rows, 2 * rows, LANES)), SHARDS)

    shapes = (((1024, BLOCK), BF16), ((512, LANES), F32), ((32, 8, LANES), F32))
    operands = (forcing,) + partners(forcing) + (rate_class, rate_table)
    lines = call(lines_kernel, "lines", shapes, operands, smem=(5,))
    own, *lines = lax.optimization_barrier((own,) + lines)
    own = own.reshape(-1, 2, rows, LANES)
    rest = partners(own)

    shapes = (((32, 3, 8, LANES), F32),) + (((BLOCK, 256), BF16),) * 2
    operands = (*lines, own, row_lines)
    out, *own = call(rows_kernel, "rows", shapes, operands)
    count = lax.axis_size(("l", "z"))
    groups = [[x * count + k for x in side for k in range(count)] for side in SIDES]
    out = swap(out, NEAR, groups)
    shapes = (((2, BLOCK, 384), BF16),) * 2
    rest = call(rest_kernel, "rest", shapes, rest)
    out, *rest = lax.optimization_barrier((out,) + rest)
    matrices = (*own, *rest)
    (out,) = call(
        middle_kernel,
        "middle",
        (((128, 8, LANES), F32),),
        (out, col_lines) + matrices,
        scratch=((2, 2, 4, 8, BLOCK), (2, 8, BLOCK)),
    )
    out = swap(out, SPREAD)
    shapes = ((forcing.shape, F32),) * 2
    return call(last_kernel, "last", shapes, (out, row_lines) + matrices)


def solution(mesh):
    devices = mesh.devices
    tm, row = devices.shape
    fine = Mesh(
        devices.reshape(tm // 2, 2, row // 16, 2, 8), ("x", "c", "h", "l", "z")
    )
    field = P(TIME, ROWS, None)
    return jax.shard_map(
        per_device,
        mesh=fine,
        in_specs=(field, P(ROWS, None), P(), P(), P(), P(None, ROWS, None)),
        out_specs=(field, field),
        check_vma=False,
    )
```

```python
import jax
import jax.numpy as jnp
from jax import lax
from jax.experimental import pallas as pl
from jax.experimental.pallas import tpu as pltpu
from jax.sharding import Mesh
from jax.sharding import PartitionSpec as P

BLOCK = 512
LANES = 128
PIECE = 32
F32 = jnp.float32
BF16 = jnp.bfloat16
ROWS = ("h", "l", "z")
TIME = ("x", "c")
NEAR = ("x", "l", "z")
SPREAD = ("z", "l", "x", "c")
SHARDS = ("z", "l", "h")
SIDES = ((0, 3), (1, 2))


def place_along_x():
    x = lax.axis_index("x")
    u = x // 2
    return u, jnp.where(lax.rem(x, 2) == u, 0, 1)


def split(values):
    high = values.astype(BF16)
    return high, (values - high.astype(F32)).astype(BF16)


def product(both, high, low, adjoint):
    dims = (((1,), (1 if adjoint else 0,)), ((), ()))
    count = both.shape[0] // 2
    wide = lax.dot_general(both, high, dims, preferred_element_type=F32)
    small = lax.dot_general(both[:count], low, dims, preferred_element_type=F32)
    return wide[:count] + (wide[count:] + small)


def own_first(lines, v, c):
    quarters = [lines[:, k * LANES : (k + 1) * LANES] for k in range(4)]
    quarters = [jnp.where(v == 0, quarters[k], quarters[(k + 2) % 4]) for k in range(4)]
    quarters = [jnp.where(c == 0, quarters[k], quarters[k ^ 1]) for k in range(4)]
    return jnp.concatenate(quarters, axis=1)


def matrix(own_ref, rest_ref, k):
    return jnp.concatenate([own_ref[:, k * LANES : (k + 1) * LANES], rest_ref[k]], axis=1)


def solve(lines, mask, matrices, adjoint):
    own_high, own_low, rest_high, rest_low = matrices
    both = jnp.concatenate(split(lines), axis=0)
    parts = []
    for k in range(2):
        high, low = matrix(own_high, rest_high, k), matrix(own_low, rest_low, k)
        parts.append(product(both, high, low, adjoint))
    return jnp.where(mask, parts[0], parts[1])


def exchange_lanes(tiles):
    group = lax.broadcasted_iota(jnp.int32, tiles[0].shape, 1) // PIECE
    out = []
    for place in range(4):
        made = None
        for source in range(4):
            turn = ((source - place) % 4) * PIECE
            rolled = pltpu.roll(tiles[source], turn, 1) if turn else tiles[source]
            made = rolled if made is None else jnp.where(group == source, rolled, made)
        out.append(made)
    return out


def class_marks(line, first, count):
    lane = lax.broadcasted_iota(jnp.int32, (count, LANES), 1)
    row = lax.broadcasted_iota(jnp.int32, (count, LANES), 0)
    picked = jnp.where((lane == row + first) & (line == 0), 1.0, 0.0)
    return jnp.sum(picked, axis=1, keepdims=True)


def row_mask(class_ref, copies):
    place = lax.axis_index(ROWS)
    line = class_ref[pl.ds(place // 4, 1), :]
    marks = class_marks(line, lax.rem(place, 4) * PIECE, PIECE)
    return jnp.concatenate([marks] * copies, axis=0) > 0.5


def lines_kernel(f0, f1, f2, f3, rate_ref, table_ref, both_ref, same_ref, decays_ref):
    quarter = place_along_x()[1] * 2 + lax.axis_index("c")
    fields = ((f0, f1), (f2, f3))
    at = [pl.multiple_of(b * BLOCK + quarter * LANES, LANES) for b in range(4)]
    for far in range(2):
        for pair in range(2):
            for core in range(2):
                for b in range(2):
                    ref, block = fields[far][core], pair * 2 + b
                    first = (((far * 2 + pair) * 2 + core) * 2 + b) * PIECE
                    rows = pl.ds(first, PIECE)
                    lines = ref[0, :, block * BLOCK : (block + 1) * BLOCK]
                    high, low = split(lines)
                    both_ref[rows, :] = high
                    both_ref[pl.ds(512 + first, PIECE), :] = low
                    same_ref[rows, :] = ref[0, :, pl.ds(at[block], LANES)]
    for pair in range(2):
        rate = [rate_ref[:, pl.ds(at[pair * 2 + b], LANES)] for b in range(2)]
        rate = jnp.concatenate(rate, axis=0)
        decays = jnp.zeros(rate.shape, F32)
        for k in range(16):
            decays = jnp.where(rate == k, table_ref[k], decays)
        decays = jnp.concatenate([decays, decays], axis=0).T.reshape(16, 8, LANES)
        decays_ref[pair * 16 : (pair + 1) * 16] = decays


def rows_kernel(
    both_ref, same_ref, decays_ref, m_ref, class_ref, out_ref, high_ref, low_ref
):
    for k in range(2):
        high, low = split(in_rows(m_ref, k))
        high_ref[:, k * LANES : (k + 1) * LANES] = high
        low_ref[:, k * LANES : (k + 1) * LANES] = low
    solved = product(both_ref[...], high_ref[...], low_ref[...], False)
    solved = jnp.where(row_mask(class_ref, 16), solved[:, :LANES], solved[:, LANES:])
    solved = solved + same_ref[...]
    for pair in range(2):
        at = slice(pair * 16, (pair + 1) * 16)
        for far in range(2):
            first = (far * 2 + pair) * LANES
            turned = solved[first : first + LANES].T
            out_ref[at, far] = turned.reshape(16, 8, LANES)
        out_ref[at, 2] = decays_ref[at]


def places(order, outer):
    step, steps = 1, {}
    for name in reversed(order):
        steps[name] = step
        step *= lax.axis_size(name)
    found = [0]
    for name in outer:
        found = [at + k * steps[name] for at in found for k in range(lax.axis_size(name))]
    return found


def in_rows(ref, k):
    pieces = [ref[at, k] for at in places(SHARDS, ROWS)]
    return jnp.concatenate(pieces, axis=0)


def rest_kernel(m1, m2, m3, high_ref, low_ref):
    for n, ref in enumerate((m1, m2, m3)):
        for k in range(2):
            high, low = split(in_rows(ref, k))
            high_ref[k, :, n * LANES : (n + 1) * LANES] = high
            low_ref[k, :, n * LANES : (n + 1) * LANES] = low


def middle_kernel(x_ref, class_ref, h0, l0, h1, l1, out_ref, a_ref, r_ref):
    c = lax.axis_index("c")
    u, v = place_along_x()
    tiles = x_ref[...].reshape(2, 4, 4, 3, 8, LANES)
    made = exchange_lanes([tiles[:, :, i, :2].reshape(128, LANES) for i in range(4)])
    for tb in range(4):
        block = made[tb].reshape(2, 4, 2, 8, LANES)
        for q in range(4):
            a_ref[:, :, tb, :, q * LANES : (q + 1) * LANES] = block[:, q]
    made = exchange_lanes([tiles[0, :, i, 2].reshape(32, LANES) for i in range(4)])
    for b in range(2):
        block = made[b].reshape(4, 8, LANES)
        for q in range(4):
            r_ref[b, :, q * LANES : (q + 1) * LANES] = block[q]
    decays = r_ref[...].reshape(16, BLOCK)
    scaled = jnp.sqrt(1.0 - decays * decays)

    place = lax.axis_index(("l", "z"))
    marks = []
    for b in range(2):
        line = class_ref[pl.ds((u * 2 + b) * 4 + v * 2 + c, 1), :]
        marks.append(class_marks(line, place * 8, 8))
    mask = jnp.concatenate(marks * 8, axis=0) > 0.5
    matrices = (h0, l0, h1, l1)
    lines = a_ref[...].reshape(128, BLOCK)
    smoothed = lines + own_first(solve(lines, mask, matrices, False), v, c)
    smoothed = smoothed.reshape(2, 2, 2, 16, BLOCK)
    state, field = None, []
    for t in range(8):
        far, late, core = t // 4, (t // 2) % 2, t % 2
        pair = smoothed[far]
        pair = jnp.where(v == far, pair[late], pair[1 - late])
        here = scaled * jnp.where(c == 0, pair[core], pair[1 - core])
        state = here if state is None else decays * state + here
        field.append(state)
    state, back = None, [None] * 8
    for t in range(7, -1, -1):
        here = scaled * field[t]
        state = here if state is None else decays * state + here
        back[t] = state
    back = jnp.concatenate(back, axis=0)
    adjoint = back + solve(own_first(back, v, c), mask, matrices, True)
    field = jnp.concatenate(field, axis=0).reshape(4, 4, 8, BLOCK)
    adjoint = adjoint.reshape(4, 4, 8, BLOCK)
    sources = places(SPREAD, ("l", "z"))
    times = places(SPREAD, TIME)
    for core in range(2):
        for q in range(4):
            lanes = slice(q * LANES, (q + 1) * LANES)
            tiles = [
                value[:, core * 2 + b, :, lanes].reshape(32, LANES)
                for value in (field, adjoint)
                for b in range(2)
            ]
            made = exchange_lanes(tiles)
            for i in range(4):
                block = made[i].reshape(4, 8, LANES)
                for x in range(4):
                    out_ref[sources[q * 4 + i] + times[x * 2 + core]] = block[x]


def last_kernel(x_ref, class_ref, h0, l0, h1, l1, field_ref, adjoint_ref):
    c = lax.axis_index("c")
    v = place_along_x()[1]
    sources = places(SPREAD, ("l", "z"))
    times = places(SPREAD, TIME)
    lines = []
    for u in range(2):
        pieces = []
        for k in range(4):
            source = (u * 2 + ((k // 2) ^ u)) * 2 + k % 2
            tiles = [x_ref[at + times[source]] for at in sources]
            turned = jnp.concatenate(tiles, axis=0).T
            for b in range(2):
                at = (u * 2 + b) * BLOCK + k * LANES
                field_ref[0, :, at : at + LANES] = turned[b * PIECE : (b + 1) * PIECE]
            pieces.append(turned[2 * PIECE :])
        lines.append(jnp.concatenate(pieces, axis=1))
    lines = jnp.concatenate(lines, axis=0)
    mask = row_mask(class_ref, 4)
    solved = lines + solve(own_first(lines, v, c), mask, (h0, l0, h1, l1), True)
    for b in range(4):
        piece = solved[b * PIECE : (b + 1) * PIECE]
        adjoint_ref[0, :, b * BLOCK : (b + 1) * BLOCK] = piece


def call(kernel, name, shapes, operands, smem=(), scratch=()):
    vmem = pl.BlockSpec(memory_space=pltpu.VMEM)
    places = [
        pl.BlockSpec(memory_space=pltpu.SMEM) if k in smem else vmem
        for k in range(len(operands))
    ]
    return pl.pallas_call(
        kernel,
        out_shape=tuple(jax.ShapeDtypeStruct(*shape) for shape in shapes),
        in_specs=places,
        out_specs=(vmem,) * len(shapes),
        scratch_shapes=[pltpu.VMEM(shape, F32) for shape in scratch],
        compiler_params=pltpu.CompilerParams(vmem_limit_bytes=40 * 1024 * 1024),
        name=name,
    )(*operands)


def swap(values, axis, groups=None):
    return lax.all_to_all(
        values, axis, split_axis=0, concat_axis=0, axis_index_groups=groups, tiled=True
    )


def partners(values):
    near = lax.ppermute(values, "x", [(k, k ^ 1) for k in range(4)])
    other = [(0, 1), (1, 0)]
    core = lax.ppermute(values, "c", other)
    return core, near, lax.ppermute(near, "c", other)


def per_device(forcing, rate_class, rate_table, row_class, col_class, offsets):
    row_lines = row_class.reshape(-1, LANES)
    col_lines = col_class.reshape(-1, LANES)

    quarter = place_along_x()[1] * 2 + lax.axis_index("c")
    rows = offsets.shape[1]
    piece = lax.dynamic_slice(offsets, (0, 0, quarter * LANES), (2, rows, LANES))
    piece = piece.reshape(2 * rows, LANES)
    own = swap(jnp.broadcast_to(piece, (BLOCK // rows, 2 * rows, LANES)), SHARDS)

    shapes = (((1024, BLOCK), BF16), ((512, LANES), F32), ((32, 8, LANES), F32))
    operands = (forcing,) + partners(forcing) + (rate_class, rate_table)
    lines = call(lines_kernel, "lines", shapes, operands, smem=(5,))
    own, *lines = lax.optimization_barrier((own,) + lines)
    own = own.reshape(-1, 2, rows, LANES)
    rest = partners(own)

    shapes = (((32, 3, 8, LANES), F32),) + (((BLOCK, 256), BF16),) * 2
    operands = (*lines, own, row_lines)
    out, *own = call(rows_kernel, "rows", shapes, operands)
    count = lax.axis_size(("l", "z"))
    groups = [[x * count + k for x in side for k in range(count)] for side in SIDES]
    out = swap(out, NEAR, groups)
    shapes = (((2, BLOCK, 384), BF16),) * 2
    rest = call(rest_kernel, "rest", shapes, rest)
    out, *rest = lax.optimization_barrier((out,) + rest)
    matrices = (*own, *rest)
    (out,) = call(
        middle_kernel,
        "middle",
        (((128, 8, LANES), F32),),
        (out, col_lines) + matrices,
        scratch=((2, 2, 4, 8, BLOCK), (2, 8, BLOCK)),
    )
    out = swap(out, SPREAD)
    shapes = ((forcing.shape, F32),) * 2
    return call(last_kernel, "last", shapes, (out, row_lines) + matrices)


def solution(mesh):
    devices = mesh.devices
    tm, row = devices.shape
    fine = Mesh(
        devices.reshape(tm // 2, 2, row // 16, 2, 8), ("x", "c", "h", "l", "z")
    )
    field = P(TIME, ROWS, None)
    return jax.shard_map(
        per_device,
        mesh=fine,
        in_specs=(field, P(ROWS, None), P(), P(), P(), P(None, ROWS, None)),
        out_specs=(field, field),
        check_vma=False,
    )
```

```python
import jax
import jax.numpy as jnp
from jax import lax
from jax.experimental import pallas as pl
from jax.experimental.pallas import tpu as pltpu
from jax.sharding import Mesh
from jax.sharding import PartitionSpec as P

BLOCK = 512
LANES = 128
PIECE = 32
F32 = jnp.float32
BF16 = jnp.bfloat16
ROWS = ("h", "l", "z")
TIME = ("x", "c")
NEAR = ("x", "l", "z")
SPREAD = ("z", "l", "x", "c")
SHARDS = ("z", "l", "h")
SIDES = ((0, 3), (1, 2))


def near_place(side, line):
    l, z = divmod(line, 8)
    return (z * 2 + l) * 2 + side


def place_along_x():
    x = lax.axis_index("x")
    u = x // 2
    return u, jnp.where(lax.rem(x, 2) == u, 0, 1)


def split(values):
    high = values.astype(BF16)
    return high, (values - high.astype(F32)).astype(BF16)


def product(both, high, low, adjoint):
    dims = (((1,), (1 if adjoint else 0,)), ((), ()))
    count = both.shape[0] // 2
    wide = lax.dot_general(both, high, dims, preferred_element_type=F32)
    small = lax.dot_general(both[:count], low, dims, preferred_element_type=F32)
    return wide[:count] + (wide[count:] + small)


def own_first(lines, v, c):
    quarters = [lines[:, k * LANES : (k + 1) * LANES] for k in range(4)]
    quarters = [jnp.where(v == 0, quarters[k], quarters[(k + 2) % 4]) for k in range(4)]
    quarters = [jnp.where(c == 0, quarters[k], quarters[k ^ 1]) for k in range(4)]
    return jnp.concatenate(quarters, axis=1)


def matrix(own_ref, rest_ref, k):
    return jnp.concatenate([own_ref[:, k * LANES : (k + 1) * LANES], rest_ref[k]], axis=1)


def solve(lines, mask, matrices, adjoint):
    own_high, own_low, rest_high, rest_low = matrices
    both = jnp.concatenate(split(lines), axis=0)
    parts = []
    for k in range(2):
        high, low = matrix(own_high, rest_high, k), matrix(own_low, rest_low, k)
        parts.append(product(both, high, low, adjoint))
    return jnp.where(mask, parts[0], parts[1])


def exchange_lanes(tiles):
    group = lax.broadcasted_iota(jnp.int32, tiles[0].shape, 1) // PIECE
    out = []
    for place in range(4):
        made = None
        for source in range(4):
            turn = ((source - place) % 4) * PIECE
            rolled = pltpu.roll(tiles[source], turn, 1) if turn else tiles[source]
            made = rolled if made is None else jnp.where(group == source, rolled, made)
        out.append(made)
    return out


def class_marks(line, first, count):
    lane = lax.broadcasted_iota(jnp.int32, (count, LANES), 1)
    row = lax.broadcasted_iota(jnp.int32, (count, LANES), 0)
    picked = jnp.where((lane == row + first) & (line == 0), 1.0, 0.0)
    return jnp.sum(picked, axis=1, keepdims=True)


def row_mask(class_ref, copies):
    place = lax.axis_index(ROWS)
    line = class_ref[pl.ds(place // 4, 1), :]
    marks = class_marks(line, lax.rem(place, 4) * PIECE, PIECE)
    return jnp.concatenate([marks] * copies, axis=0) > 0.5


def lines_kernel(f0, f1, f2, f3, rate_ref, table_ref, both_ref, same_ref, decays_ref):
    quarter = place_along_x()[1] * 2 + lax.axis_index("c")
    fields = ((f0, f1), (f2, f3))
    at = [pl.multiple_of(b * BLOCK + quarter * LANES, LANES) for b in range(4)]
    for far in range(2):
        for pair in range(2):
            for core in range(2):
                for b in range(2):
                    ref, block = fields[far][core], pair * 2 + b
                    first = (((far * 2 + pair) * 2 + core) * 2 + b) * PIECE
                    rows = pl.ds(first, PIECE)
                    lines = ref[0, :, block * BLOCK : (block + 1) * BLOCK]
                    high, low = split(lines)
                    both_ref[rows, :] = high
                    both_ref[pl.ds(512 + first, PIECE), :] = low
                    same_ref[rows, :] = ref[0, :, pl.ds(at[block], LANES)]
    for pair in range(2):
        rate = [rate_ref[:, pl.ds(at[pair * 2 + b], LANES)] for b in range(2)]
        rate = jnp.concatenate(rate, axis=0)
        decays = jnp.zeros(rate.shape, F32)
        for k in range(16):
            decays = jnp.where(rate == k, table_ref[k], decays)
        decays = jnp.concatenate([decays, decays], axis=0).T.reshape(16, 8, LANES)
        decays_ref[pair * 16 : (pair + 1) * 16] = decays


def rows_kernel(
    both_ref, same_ref, decays_ref, m_ref, class_ref, out_ref, high_ref, low_ref
):
    for k in range(2):
        high, low = split(in_rows(m_ref, k))
        high_ref[:, k * LANES : (k + 1) * LANES] = high
        low_ref[:, k * LANES : (k + 1) * LANES] = low
    solved = product(both_ref[...], high_ref[...], low_ref[...], False)
    solved = jnp.where(row_mask(class_ref, 16), solved[:, :LANES], solved[:, LANES:])
    solved = solved + same_ref[...]
    for pair in range(2):
        for far in range(2):
            first = (far * 2 + pair) * LANES
            turned = solved[first : first + LANES].T.reshape(16, 8, LANES)
            for line in range(16):
                out_ref[near_place(pair, line), far] = turned[line]
        for line in range(16):
            out_ref[near_place(pair, line), 2] = decays_ref[pair * 16 + line]


def places(order, outer):
    step, steps = 1, {}
    for name in reversed(order):
        steps[name] = step
        step *= lax.axis_size(name)
    found = [0]
    for name in outer:
        found = [at + k * steps[name] for at in found for k in range(lax.axis_size(name))]
    return found


def in_rows(ref, k):
    pieces = [ref[at, k] for at in places(SHARDS, ROWS)]
    return jnp.concatenate(pieces, axis=0)


def rest_kernel(m1, m2, m3, high_ref, low_ref):
    for n, ref in enumerate((m1, m2, m3)):
        for k in range(2):
            high, low = split(in_rows(ref, k))
            high_ref[k, :, n * LANES : (n + 1) * LANES] = high
            low_ref[k, :, n * LANES : (n + 1) * LANES] = low


def middle_kernel(x_ref, class_ref, h0, l0, h1, l1, out_ref, a_ref, r_ref):
    c = lax.axis_index("c")
    u, v = place_along_x()
    tiles = []
    for i in range(4):
        found = [near_place(side, q * 4 + i) for side in range(2) for q in range(4)]
        tiles.append(jnp.concatenate([x_ref[at, :2] for at in found], axis=0))
    made = exchange_lanes([tile.reshape(128, LANES) for tile in tiles])
    for tb in range(4):
        block = made[tb].reshape(2, 4, 2, 8, LANES)
        for q in range(4):
            a_ref[:, :, tb, :, q * LANES : (q + 1) * LANES] = block[:, q]
    tiles = []
    for i in range(4):
        found = [near_place(0, q * 4 + i) for q in range(4)]
        tiles.append(jnp.concatenate([x_ref[at, 2] for at in found], axis=0))
    made = exchange_lanes(tiles)
    for b in range(2):
        block = made[b].reshape(4, 8, LANES)
        for q in range(4):
            r_ref[b, :, q * LANES : (q + 1) * LANES] = block[q]
    decays = r_ref[...].reshape(16, BLOCK)
    scaled = jnp.sqrt(1.0 - decays * decays)

    place = lax.axis_index(("l", "z"))
    marks = []
    for b in range(2):
        line = class_ref[pl.ds((u * 2 + b) * 4 + v * 2 + c, 1), :]
        marks.append(class_marks(line, place * 8, 8))
    mask = jnp.concatenate(marks * 8, axis=0) > 0.5
    matrices = (h0, l0, h1, l1)
    lines = a_ref[...].reshape(128, BLOCK)
    smoothed = lines + own_first(solve(lines, mask, matrices, False), v, c)
    smoothed = smoothed.reshape(2, 2, 2, 16, BLOCK)
    state, field = None, []
    for t in range(8):
        far, late, core = t // 4, (t // 2) % 2, t % 2
        pair = smoothed[far]
        pair = jnp.where(v == far, pair[late], pair[1 - late])
        here = scaled * jnp.where(c == 0, pair[core], pair[1 - core])
        state = here if state is None else decays * state + here
        field.append(state)
    state, back = None, [None] * 8
    for t in range(7, -1, -1):
        here = scaled * field[t]
        state = here if state is None else decays * state + here
        back[t] = state
    back = jnp.concatenate(back, axis=0)
    adjoint = back + solve(own_first(back, v, c), mask, matrices, True)
    field = jnp.concatenate(field, axis=0).reshape(4, 4, 8, BLOCK)
    adjoint = adjoint.reshape(4, 4, 8, BLOCK)
    sources = places(SPREAD, ("l", "z"))
    times = places(SPREAD, TIME)
    for core in range(2):
        for q in range(4):
            lanes = slice(q * LANES, (q + 1) * LANES)
            tiles = [
                value[:, core * 2 + b, :, lanes].reshape(32, LANES)
                for value in (field, adjoint)
                for b in range(2)
            ]
            made = exchange_lanes(tiles)
            for i in range(4):
                block = made[i].reshape(4, 8, LANES)
                for x in range(4):
                    out_ref[sources[q * 4 + i] + times[x * 2 + core]] = block[x]


def last_kernel(x_ref, class_ref, h0, l0, h1, l1, field_ref, adjoint_ref):
    c = lax.axis_index("c")
    v = place_along_x()[1]
    sources = places(SPREAD, ("l", "z"))
    times = places(SPREAD, TIME)
    lines = []
    for u in range(2):
        pieces = []
        for k in range(4):
            source = (u * 2 + ((k // 2) ^ u)) * 2 + k % 2
            tiles = [x_ref[at + times[source]] for at in sources]
            turned = jnp.concatenate(tiles, axis=0).T
            for b in range(2):
                at = (u * 2 + b) * BLOCK + k * LANES
                field_ref[0, :, at : at + LANES] = turned[b * PIECE : (b + 1) * PIECE]
            pieces.append(turned[2 * PIECE :])
        lines.append(jnp.concatenate(pieces, axis=1))
    lines = jnp.concatenate(lines, axis=0)
    mask = row_mask(class_ref, 4)
    solved = lines + solve(own_first(lines, v, c), mask, (h0, l0, h1, l1), True)
    for b in range(4):
        piece = solved[b * PIECE : (b + 1) * PIECE]
        adjoint_ref[0, :, b * BLOCK : (b + 1) * BLOCK] = piece


def call(kernel, name, shapes, operands, smem=(), scratch=()):
    vmem = pl.BlockSpec(memory_space=pltpu.VMEM)
    places = [
        pl.BlockSpec(memory_space=pltpu.SMEM) if k in smem else vmem
        for k in range(len(operands))
    ]
    return pl.pallas_call(
        kernel,
        out_shape=tuple(jax.ShapeDtypeStruct(*shape) for shape in shapes),
        in_specs=places,
        out_specs=(vmem,) * len(shapes),
        scratch_shapes=[pltpu.VMEM(shape, F32) for shape in scratch],
        compiler_params=pltpu.CompilerParams(vmem_limit_bytes=40 * 1024 * 1024),
        name=name,
    )(*operands)


def swap(values, axis, groups=None):
    return lax.all_to_all(
        values, axis, split_axis=0, concat_axis=0, axis_index_groups=groups, tiled=True
    )


def partners(values):
    near = lax.ppermute(values, "x", [(k, k ^ 1) for k in range(4)])
    other = [(0, 1), (1, 0)]
    core = lax.ppermute(values, "c", other)
    return core, near, lax.ppermute(near, "c", other)


def per_device(forcing, rate_class, rate_table, row_class, col_class, offsets):
    row_lines = row_class.reshape(-1, LANES)
    col_lines = col_class.reshape(-1, LANES)

    quarter = place_along_x()[1] * 2 + lax.axis_index("c")
    rows = offsets.shape[1]
    piece = lax.dynamic_slice(offsets, (0, 0, quarter * LANES), (2, rows, LANES))
    piece = piece.reshape(2 * rows, LANES)
    own = swap(jnp.broadcast_to(piece, (BLOCK // rows, 2 * rows, LANES)), SHARDS)

    shapes = (((1024, BLOCK), BF16), ((512, LANES), F32), ((32, 8, LANES), F32))
    operands = (forcing,) + partners(forcing) + (rate_class, rate_table)
    lines = call(lines_kernel, "lines", shapes, operands, smem=(5,))
    own, *lines = lax.optimization_barrier((own,) + lines)
    own = own.reshape(-1, 2, rows, LANES)
    rest = partners(own)

    shapes = (((32, 3, 8, LANES), F32),) + (((BLOCK, 256), BF16),) * 2
    operands = (*lines, own, row_lines)
    out, *own = call(rows_kernel, "rows", shapes, operands)
    count = lax.axis_size(("l", "z"))
    groups = []
    for side in SIDES:
        lines = [l * 8 + z for z in range(8) for l in range(2)]
        groups.append([x * count + line for line in lines for x in side])
    out = swap(out, NEAR, groups)
    shapes = (((2, BLOCK, 384), BF16),) * 2
    rest = call(rest_kernel, "rest", shapes, rest)
    out, *rest = lax.optimization_barrier((out,) + rest)
    matrices = (*own, *rest)
    (out,) = call(
        middle_kernel,
        "middle",
        (((128, 8, LANES), F32),),
        (out, col_lines) + matrices,
        scratch=((2, 2, 4, 8, BLOCK), (2, 8, BLOCK)),
    )
    out = swap(out, SPREAD)
    shapes = ((forcing.shape, F32),) * 2
    return call(last_kernel, "last", shapes, (out, row_lines) + matrices)


def solution(mesh):
    devices = mesh.devices
    tm, row = devices.shape
    fine = Mesh(
        devices.reshape(tm // 2, 2, row // 16, 2, 8), ("x", "c", "h", "l", "z")
    )
    field = P(TIME, ROWS, None)
    return jax.shard_map(
        per_device,
        mesh=fine,
        in_specs=(field, P(ROWS, None), P(), P(), P(), P(None, ROWS, None)),
        out_specs=(field, field),
        check_vma=False,
    )
```
